256 devices in a mesh: long: 16 (over y, x_hi, core), inner: 16 (over x_lo, z).
Axes of the slice: x: 4 (x_hi: 2, x_lo: 2; x = x_hi * 2 + x_lo), y: 4, z: 8, core: 2. Of those that a mesh axis runs over, the one named last changes fastest.
Arguments:
- image_raw: bfloat16 [16384, 1280], P(('long', 'inner')), may hold values from -1 to 1, as said below
- text_raw: bfloat16 [16384, 1280], P(('long', 'inner')), may hold values from -1 to 1, as said below
- log_scale: float32 [1], replicated, may hold values from 4 to 4.6
Outputs:
- grad_image: bfloat16 [16384, 1280], P(('long', 'inner'))
- grad_text: bfloat16 [16384, 1280], P(('long', 'inner'))
- loss: float32 [1], replicated
- grad_log_scale: float32 [1], replicated
The draws below stay inside these ranges and needn't reach their ends.
Inputs may be any that keep to these rules, and one draw needn't show every extreme that they name: `image_raw`: each image row and its paired text row are partly aligned. `text_raw`: each text row and its paired image row are partly aligned.
All inputs are finite; a program needn't handle non-finite values.
Results may differ from the reference program's by a relative error of at most 0.017.
Values may be sent and summed in bfloat16 or wider, within the bound.
No kernel may reach another device: no remote copies, remote signals or barrier semaphores. Data moves between devices by JAX's collectives and lax.ppermute only.
A program may use at most 64 MiB of HBM per device.

```python
import math
import jax
import jax.numpy as jnp
from jax import lax

E = 1280
BATCH = 16384


def common_draw(key, strong_share, strong_align):
    first_key, second_key, third_key = jax.random.split(key, 3)
    shared = jax.random.truncated_normal(first_key, -5.0, 5.0, (BATCH, E), jnp.float32)
    alignment = jax.random.uniform(second_key, (BATCH, 1), jnp.float32, 0.3, 0.5)
    picked = jax.random.uniform(third_key, (BATCH, 1), jnp.float32) < strong_share
    alignment = jnp.where(picked, strong_align, alignment)
    return (shared, alignment)


def mixed_rows(key, shared, alignment, spread):
    noise_key, scale_key = jax.random.split(key, 2)
    noise_part = jax.random.truncated_normal(noise_key, -5.0, 5.0, (BATCH, E), jnp.float32)
    row_scale = jnp.exp(jax.random.uniform(scale_key, (BATCH, 1), jnp.float32, -spread, spread))
    values = (alignment * shared + jnp.sqrt(1.0 - alignment * alignment) * noise_part) * row_scale / math.sqrt(E)
    values = jnp.clip(values, -1.0, 1.0)
    return values.astype(jnp.bfloat16)


def draw_image_raw(key, part):
    shared, alignment = common_draw(key, 0.0, 0.5)
    spread = math.log(2.0)
    key = jax.random.fold_in(key, 1)
    return mixed_rows(key, shared, alignment, spread)


def draw_text_raw(key, part):
    shared, alignment = common_draw(key, 0.0, 0.5)
    spread = math.log(2.0)
    key = jax.random.fold_in(key, 2)
    return mixed_rows(key, shared, alignment, spread)


def setup_inputs(seed: int = 0) -> dict:
    key_list = jax.random.split(jax.random.key(seed), 4)
    return {
        "image_raw": draw_image_raw(jax.random.fold_in(key_list[3], 71), 0),
        "text_raw": draw_text_raw(jax.random.fold_in(key_list[3], 71), 0),
        "log_scale": jnp.clip(jax.random.uniform(key_list[2], (1,), jnp.float32, 4.0, 4.6), 4.0, 4.6),
    }


NORM_EPS = 1e-06

def normalize(raw_rows):
    values = raw_rows.astype(jnp.float32)
    inv_norm = 1.0 / jnp.sqrt(lax.optimization_barrier(jnp.sum(values * values, axis=1, keepdims=True)) + NORM_EPS)
    return (values * inv_norm, inv_norm)

def unnormalize(grad_hat, unit_rows, inv_norm):
    inner_prod = lax.optimization_barrier(jnp.sum(grad_hat * unit_rows, axis=1, keepdims=True))
    return (inv_norm * (grad_hat - unit_rows * inner_prod)).astype(jnp.bfloat16)

def reference(image_raw, text_raw, log_scale):
    img_unit, img_norm = normalize(image_raw)
    txt_unit, txt_norm = normalize(text_raw)
    img_hat = img_unit.astype(jnp.bfloat16)
    txt_hat = txt_unit.astype(jnp.bfloat16)
    logit_mult = jnp.exp(log_scale[0])
    logits = logit_mult * jnp.dot(img_hat, txt_hat.T, preferred_element_type=jnp.float32)
    lse_row = jax.nn.logsumexp(logits, axis=1)
    lse_col = jax.nn.logsumexp(logits, axis=0)
    diagonal = jnp.diagonal(logits)
    loss_value = (jnp.sum(lse_row - diagonal) + jnp.sum(lse_col - diagonal)) / (2 * BATCH)
    dlogits = 0.5 * jnp.exp(logits - lse_row[:, None]) + 0.5 * jnp.exp(logits - lse_col[None, :]) - jnp.eye(BATCH, dtype=jnp.float32)
    scale_grad = jnp.sum(dlogits * logits) / BATCH
    dlogits_b = dlogits.astype(jnp.bfloat16)
    grad_img_hat = logit_mult * jnp.dot(dlogits_b, txt_hat, preferred_element_type=jnp.float32)
    grad_txt_hat = logit_mult * jnp.dot(dlogits_b.T, img_hat, preferred_element_type=jnp.float32)
    grad_image = unnormalize(grad_img_hat, img_unit, img_norm)
    grad_text = unnormalize(grad_txt_hat, txt_unit, txt_norm)
    return (grad_image, grad_text, jnp.reshape(loss_value, (1,)), jnp.reshape(scale_grad, (1,)))
```

```python
import functools
import itertools

import jax
import jax.numpy as jnp
from jax import lax
from jax.experimental import pallas as pl
from jax.experimental.pallas import tpu as pltpu
from jax.sharding import Mesh, PartitionSpec as P

NORM_EPS = 1e-06
AXES = ("y", "xh", "c", "xl", "z")
SIZES = (4, 2, 2, 2, 8)
PLANE = ("y", "xh", "xl")
LINE = ("c", "z")
GROUP = 16
VMEM_LIMIT = 48 * 1024 * 1024
F32 = jnp.float32
BF16 = jnp.bfloat16


def params():
    return pltpu.CompilerParams(vmem_limit_bytes=VMEM_LIMIT)


def whole(space=pltpu.VMEM):
    return pl.BlockSpec(memory_space=space)


def permute(array, move):
    pairs = []
    for y, xh, c, xl, z in itertools.product(*map(range, SIZES)):
        x, y2, z2, c2 = move(2 * xh + xl, y, z, c)
        x, y2, z2, c2 = x % 4, y2 % 4, z2 % 8, c2 % 2
        flat = lambda y, x, z, c: (((y * 2 + x // 2) * 2 + c) * 2 + x % 2) * 8 + z
        pairs.append((flat(y, 2 * xh + xl, z, c), flat(y2, x, z2, c2)))
    return lax.ppermute(array, AXES, pairs)


def plane_step(step, turned):
    def move(x, y, z, c):
        return (x + step, y, z, c) if (c == 0) != turned else (x, y + step, z, c)

    return move


def ring_gather(block, turned):
    half = block.shape[0] // 2
    below = permute(block, plane_step(1, turned))
    above = permute(block, plane_step(-1, turned))
    far_low = permute(below[:half], plane_step(1, turned))
    far_high = permute(above[half:], plane_step(-1, turned))
    return [block, below, above, far_low, far_high]


def normalize_kernel(img_ref, txt_ref, img_hat_ref, txt_hat_ref, diag_ref):
    hats = []
    for raw, hat in ((img_ref, img_hat_ref), (txt_ref, txt_hat_ref)):
        values = raw[...].astype(F32)
        recip = 1.0 / jnp.sqrt(jnp.sum(values * values, axis=1, keepdims=True) + NORM_EPS)
        hat[...] = (values * recip).astype(BF16)
        hats.append(hat[...].astype(F32))
    diag = jnp.sum(hats[0] * hats[1])
    diag_ref[...] = jnp.full(diag_ref.shape, diag, F32)


def rows_of(vector):
    return jnp.concatenate([vector[:, k * 128 : (k + 1) * 128] for k in range(8)], axis=0)


def lanes_of(rows):
    return jnp.concatenate([rows[k : k + 1, :] for k in range(8)], axis=1)


def logits_kernel(tile, place_ref, scale_ref, img_ref, t0, t1, t2, t3, t4, txt_ref, logit_ref, row_ref, col_ref, txt_all, row_acc):
    step = pl.program_id(0)
    steps = pl.num_programs(0)

    @pl.when(step == 0)
    def _():
        pieces = [(t0, 0), (t0, 1), (t0, 2), (t0, 3), (t1, 0), (t1, 1), (t1, 2), (t1, 3)]
        pieces += [(t2, 0), (t2, 1), (t2, 2), (t2, 3), (t3, 0), (t3, 1), (t4, 0), (t4, 1)]
        for k, (ref, at) in enumerate(pieces):
            start = pl.multiple_of(place_ref[k] * 64, 64)
            txt_all[pl.ds(start, 64), :] = ref[at * 64 : (at + 1) * 64, :]
        txt_ref[...] = txt_all[...]
        row_acc[...] = jnp.zeros_like(row_acc)

    scale = scale_ref[0]
    shift = scale_ref[1]
    start = pl.multiple_of(step * tile, tile)
    block = txt_all[pl.ds(start, tile), :]
    logits = scale * lax.dot_general(img_ref[...], block, (((1,), (1,)), ((), ())), preferred_element_type=F32)
    logit_ref[...] = logits
    powers = jnp.exp(logits - shift)
    weighted = powers * logits
    for k in range(tile // 128):
        row_acc[0] += powers[:, k * 128 : (k + 1) * 128]
        row_acc[1] += weighted[:, k * 128 : (k + 1) * 128]
    sums = jnp.sum(powers, axis=0, keepdims=True)
    slopes = jnp.sum(weighted, axis=0, keepdims=True)
    rows = tile // 128
    for k in range(rows):
        for copy in range(GROUP):
            col_ref[copy, pl.ds(step * rows + k, 1), :] = sums[:, k * 128 : (k + 1) * 128]
            col_ref[copy, pl.ds(8 + step * rows + k, 1), :] = slopes[:, k * 128 : (k + 1) * 128]

    @pl.when(step == steps - 1)
    def _():
        row_ref[0:8, :] = rows_of(jnp.sum(row_acc[0].T, axis=0, keepdims=True))
        row_ref[8:16, :] = rows_of(jnp.sum(row_acc[1].T, axis=0, keepdims=True))


def column_kernel(col_ref, row_ref, diag_ref, send_ref, sums_ref):
    total = jnp.sum(col_ref[...], axis=0)
    sums, slopes = total[0:8], total[8:16]
    sums_ref[...] = sums
    log_sum = jnp.sum(jnp.log(sums))
    slope_sum = 0.5 * jnp.sum(slopes / sums)
    lane = lax.broadcasted_iota(jnp.int32, (8, 128), 1)
    scalars = jnp.where(lane == 0, log_sum, jnp.where(lane == 1, slope_sum, diag_ref[...]))
    for copy in range(GROUP):
        send_ref[copy, 0:16, :] = row_ref[...]
        send_ref[copy, 16:24, :] = scalars


def image_kernel(tile, core_ref, shift_ref, logit_ref, txt_ref, recv_ref, sums_ref, keep_ref, send_ref, dlogit_ref, scalar_ref, row_half, col_half):
    step = pl.program_id(0)

    @pl.when(step == 0)
    def _():
        total = jnp.sum(recv_ref[...], axis=0)
        sums, slopes, others = total[0:8], total[8:16], total[16:24]
        log_sum = jnp.sum(jnp.log(sums))
        slope_sum = 0.5 * jnp.sum(slopes / sums)
        lane = lax.broadcasted_iota(jnp.int32, (8, 128), 1)
        row = lax.broadcasted_iota(jnp.int32, (8, 128), 0)
        own = jnp.where(lane == 0, log_sum, jnp.where(lane == 1, slope_sum, others))
        scalar_ref[...] = jnp.where(row == 0, others, own)
        row_half[...] = jnp.broadcast_to(lanes_of(0.5 / sums), (128, 1024)).T
        col_half[...] = lanes_of(0.5 / sums_ref[...])

    start = pl.multiple_of(step * tile, tile)
    powers = jnp.exp(logit_ref[...] - shift_ref[1])
    by_row = row_half[pl.ds(start, tile), :]
    by_row = jnp.concatenate([by_row] * 8, axis=1)
    dlogit = (powers * (by_row + col_half[...])).astype(BF16)
    dlogit_ref[...] = dlogit
    grad = jnp.dot(dlogit, txt_ref[...], preferred_element_type=F32).astype(BF16)
    half = 512 // tile
    mine = (step // half) == core_ref[0]
    inside = pl.multiple_of(lax.rem(step, half) * tile, tile)

    @pl.when(mine)
    def _():
        keep_ref[pl.ds(inside, tile), :] = grad

    @pl.when(jnp.logical_not(mine))
    def _():
        send_ref[pl.ds(inside, tile), :] = grad


def text_kernel(dlogit_ref, img_ref, grad_ref):
    grad_ref[...] = lax.dot_general(
        dlogit_ref[...], img_ref[...], (((0,), (0,)), ((), ())), preferred_element_type=F32
    ).astype(BF16)


def add_kernel(a_ref, b_ref, out_ref):
    out_ref[...] = (a_ref[...].astype(F32) + b_ref[...].astype(F32)).astype(BF16)


def final_kernel(scale_ref, img_ref, txt_ref, img_hat_ref, txt_hat_ref, img_sum_ref, txt_parts_ref, grad_img_ref, grad_txt_ref):
    scale = scale_ref[0]
    txt_sum = jnp.sum(txt_parts_ref[...].astype(F32), axis=0)
    for raw, other, total, out in (
        (img_ref, txt_hat_ref, img_sum_ref[...].astype(F32), grad_img_ref),
        (txt_ref, img_hat_ref, txt_sum, grad_txt_ref),
    ):
        values = raw[...].astype(F32)
        recip = 1.0 / jnp.sqrt(jnp.sum(values * values, axis=1, keepdims=True) + NORM_EPS)
        unit = values * recip
        grad_hat = scale * (total - other[...].astype(F32))
        inner = jnp.sum(grad_hat * unit, axis=1, keepdims=True)
        out[...] = (recip * (grad_hat - unit * inner)).astype(BF16)


def per_device(image_raw, text_raw, log_scale):
    rows, width = image_raw.shape
    total = rows * GROUP
    shape = jax.ShapeDtypeStruct
    img_hat, txt_hat, diag = pl.pallas_call(
        normalize_kernel,
        out_shape=(shape((rows, width), BF16), shape((rows, width), BF16), shape((8, 128), F32)),
        in_specs=[whole()] * 2,
        out_specs=(whole(),) * 3,
        compiler_params=params(),
        name="normalize",
    )(image_raw, text_raw)

    scale = jnp.exp(log_scale[0])
    shift = jnp.maximum(1.01 * scale - 70.0, 0.0)
    scales = jnp.stack([scale, shift])
    core = lax.axis_index("c")
    my_y = lax.axis_index("y")
    my_x = 2 * lax.axis_index("xh") + lax.axis_index("xl")
    near = jnp.array([0, 3, 1, 2], jnp.int32)
    first = jnp.tile(near, 4)
    second = jnp.repeat(near, 4)
    on_x = jnp.where(core == 0, first, second)
    on_y = jnp.where(core == 0, second, first)
    place = ((my_y + on_y) % 4) * 4 + (my_x + on_x) % 4
    core_id = jnp.reshape(core, (1,)).astype(jnp.int32)

    img_all = lax.all_gather(img_hat, LINE, axis=0, tiled=True)
    line = jnp.concatenate(ring_gather(txt_hat, False), axis=0)
    pieces = ring_gather(line, True)

    tile = 256
    steps = total // tile
    fixed = lambda *block: pl.BlockSpec(block, lambda i: (0,) * len(block))
    txt_all, logits, row_part, col_part = pl.pallas_call(
        functools.partial(logits_kernel, tile),
        grid=(steps,),
        out_shape=(
            shape((total, width), BF16),
            shape((total, total), F32),
            shape((16, 128), F32),
            shape((GROUP, 16, 128), F32),
        ),
        in_specs=[whole(pltpu.SMEM), whole(pltpu.SMEM), fixed(total, width)]
        + [fixed(*piece.shape) for piece in pieces],
        out_specs=(
            fixed(total, width),
            pl.BlockSpec((total, tile), lambda i: (0, i)),
            fixed(16, 128),
            fixed(GROUP, 16, 128),
        ),
        scratch_shapes=[pltpu.VMEM((total, width), BF16), pltpu.VMEM((2, total, 128), F32)],
        compiler_params=params(),
        name="logits",
    )(place, scales, img_all, *pieces)

    col_recv = lax.all_to_all(col_part, PLANE, 0, 0, tiled=True)
    row_send, col_sums = pl.pallas_call(
        column_kernel,
        out_shape=(shape((GROUP, 24, 128), F32), shape((8, 128), F32)),
        in_specs=[whole()] * 3,
        out_specs=(whole(),) * 2,
        compiler_params=params(),
        name="columns",
    )(col_recv, row_part, diag)
    row_recv = lax.all_to_all(row_send, LINE, 0, 0, tiled=True)

    keep, send, dlogits, scalars = pl.pallas_call(
        functools.partial(image_kernel, tile),
        grid=(steps,),
        out_shape=(
            shape((total // 2, width), BF16),
            shape((total // 2, width), BF16),
            shape((total, total), BF16),
            shape((8, 128), F32),
        ),
        in_specs=[
            whole(pltpu.SMEM),
            whole(pltpu.SMEM),
            pl.BlockSpec((tile, total), lambda i: (i, 0)),
            fixed(total, width),
            fixed(GROUP, 24, 128),
            fixed(8, 128),
        ],
        out_specs=(
            fixed(total // 2, width),
            fixed(total // 2, width),
            pl.BlockSpec((tile, total), lambda i: (i, 0)),
            fixed(8, 128),
        ),
        scratch_shapes=[pltpu.VMEM((total, 128), F32), pltpu.VMEM((1, total), F32)],
        compiler_params=params(),
        name="image_grad",
    )(core_id, scales, logits, txt_all, row_recv, col_sums)

    sibling = permute(send, lambda x, y, z, c: (x, y, z, c + 1))
    txt_part = pl.pallas_call(
        text_kernel,
        grid=(steps,),
        out_shape=shape((total, width), BF16),
        in_specs=[pl.BlockSpec((total, tile), lambda i: (0, i)), fixed(total, width)],
        out_specs=pl.BlockSpec((tile, width), lambda i: (i, 0)),
        compiler_params=params(),
        cost_estimate=pl.CostEstimate(flops=2 * total * total * width, bytes_accessed=8 << 20, transcendentals=0),
        name="text_grad",
    )(dlogits, img_all)
    both = pl.pallas_call(
        add_kernel,
        out_shape=shape((total // 2, width), BF16),
        in_specs=[whole()] * 2,
        out_specs=whole(),
        compiler_params=params(),
        name="add",
    )(keep, sibling)
    img_sum = lax.psum_scatter(both, "z", scatter_dimension=0, tiled=True)
    txt_parts = lax.all_to_all(jnp.reshape(txt_part, (GROUP, rows, width)), PLANE, 0, 0, tiled=True)

    part = scalars[1:2]
    for along in ("x", "y"):
        moved = [
            permute(part, lambda x, y, z, c, k=k: (x + k, y, z, c) if along == "x" else (x, y + k, z, c))
            for k in (1, 2, 3)
        ]
        part = part + moved[0] + moved[1] + moved[2]

    grad_image, grad_text = pl.pallas_call(
        final_kernel,
        out_shape=(shape((rows, width), BF16),) * 2,
        in_specs=[whole(pltpu.SMEM)] + [whole()] * 6,
        out_specs=(whole(),) * 2,
        compiler_params=params(),
        name="finish",
    )(scales, image_raw, text_raw, img_hat, txt_hat, img_sum, txt_parts)
    batch = total * GROUP
    diag_sum = scale * part[0, 2]
    logs = scalars[0, 0] + part[0, 0] + 2.0 * batch * shift
    loss = (logs - 2.0 * diag_sum) / (2 * batch)
    slope = (scalars[0, 1] + part[0, 1] - diag_sum) / batch
    return grad_image, grad_text, jnp.reshape(loss, (1,)), jnp.reshape(slope, (1,))


def solution(mesh):
    mesh = Mesh(mesh.devices.reshape(SIZES), AXES)
    spec = P(AXES, None)
    return jax.shard_map(
        per_device, mesh=mesh, in_specs=(spec, spec, P()), out_specs=(spec, spec, P(), P()), check_vma=False
    )
```

```python
import itertools

import jax
import jax.numpy as jnp
from jax import lax
from jax.experimental import pallas as pl
from jax.experimental.pallas import tpu as pltpu
from jax.sharding import Mesh, PartitionSpec as P

NORM_EPS = 1e-06
AXES = ("y", "xh", "c", "xl", "z")
SIZES = (4, 2, 2, 2, 8)
GROUP = 16
ROWS = 64
VMEM_LIMIT = 40 * 1024 * 1024
F32 = jnp.float32
BF16 = jnp.bfloat16
VMEM = pl.BlockSpec(memory_space=pltpu.VMEM)
SMEM = pl.BlockSpec(memory_space=pltpu.SMEM)


def call(kernel, out, ins, name, flops=0, **more):
    return pl.pallas_call(
        kernel,
        out_shape=out,
        in_specs=ins,
        compiler_params=pltpu.CompilerParams(vmem_limit_bytes=VMEM_LIMIT),
        cost_estimate=pl.CostEstimate(flops=flops, bytes_accessed=1 << 20, transcendentals=0),
        name=name,
        **more,
    )


def shape(*dims, dtype=BF16):
    return jax.ShapeDtypeStruct(dims, dtype)


def permute(array, move):
    flat = lambda x, y, z, c: (((y * 2 + x // 2) * 2 + c) * 2 + x % 2) * 8 + z
    pairs = []
    for y, xh, c, xl, z in itertools.product(*map(range, SIZES)):
        x2, y2, z2, c2 = move(2 * xh + xl, y, z, c)
        pairs.append((flat(2 * xh + xl, y, z, c), flat(x2 % 4, y2 % 4, z2 % 8, c2 % 2)))
    return lax.ppermute(array, AXES, pairs)


def to_sibling(array):
    return permute(array, lambda x, y, z, c: (x, y, z, 1 - c))


def along(array, axis, step):
    steps = {"x": (step, 0, 0), "y": (0, step, 0), "z": (0, 0, step)}[axis]
    return permute(array, lambda x, y, z, c: (x + steps[0], y + steps[1], z + steps[2], c))


def first_axis(array, step):
    return permute(array, lambda x, y, z, c: (x + step, y, z, c) if c == 0 else (x, y + step, z, c))


def second_axis(array, step):
    return permute(array, lambda x, y, z, c: (x, y + step, z, c) if c == 0 else (x + step, y, z, c))


def ring(array, step):
    return permute(array, lambda x, y, z, c: (x, y, z + (step if c == 0 else -step), c))


def add(*arrays):
    return sum(array.astype(F32) for array in arrays).astype(BF16)


def normalize_kernel(img_ref, txt_ref, img_hat_ref, txt_hat_ref, diag_ref):
    hats = []
    for raw, hat in ((img_ref, img_hat_ref), (txt_ref, txt_hat_ref)):
        values = raw[...].astype(F32)
        recip = 1.0 / jnp.sqrt(jnp.sum(values * values, axis=1, keepdims=True) + NORM_EPS)
        hat[...] = (values * recip).astype(BF16)
        hats.append(hat[...].astype(F32))
    diag_ref[...] = jnp.full(diag_ref.shape, jnp.sum(hats[0] * hats[1]), F32)


def logits_kernel(*refs):
    row_place, col_place, scale_ref, diag_ref = refs[:4]
    img_refs, txt_refs = refs[4:20], refs[20:28]
    img_all, txt_all, logit_ref, row_ref, col_ref, row_acc = refs[28:]
    step = pl.program_id(0)
    tile = logit_ref.shape[1]

    @pl.when(step == 0)
    def _():
        for k, ref in enumerate(img_refs):
            img_all[k * 64 : (k + 1) * 64, :] = ref[...]
        for k, ref in enumerate(txt_refs):
            txt_all[k * 128 : (k + 1) * 128, :] = ref[...]
        row_acc[...] = jnp.zeros_like(row_acc)

    start = pl.multiple_of(step * tile, tile)
    block = txt_all[pl.ds(start, tile), :]
    logits = scale_ref[0] * lax.dot_general(
        img_all[...], block, (((1,), (1,)), ((), ())), preferred_element_type=F32
    )
    logit_ref[...] = logits
    powers = jnp.exp(logits - scale_ref[1])
    weighted = powers * logits
    for k in range(tile // 128):
        row_acc[0] += powers[:, k * 128 : (k + 1) * 128]
        row_acc[1] += weighted[:, k * 128 : (k + 1) * 128]
    sums = jnp.sum(powers, axis=0, keepdims=True)
    slopes = jnp.sum(weighted, axis=0, keepdims=True)
    for k in range(tile // 64):
        at = col_place[step * (tile // 64) + k]
        cut = slice(k * 64, (k + 1) * 64)
        col_ref[pl.ds(at, 1), :] = jnp.concatenate([sums[:, cut], slopes[:, cut]], axis=1)

    @pl.when(step == pl.num_programs(0) - 1)
    def _():
        sums = jnp.sum(row_acc[0].T, axis=0, keepdims=True)
        slopes = jnp.sum(row_acc[1].T, axis=0, keepdims=True)
        for k in range(GROUP):
            cut = slice(k * 64, (k + 1) * 64)
            row_ref[pl.ds(row_place[k], 1), :] = jnp.concatenate([sums[:, cut], slopes[:, cut]], axis=1)
        row_ref[16:24, :] = diag_ref[...]


def grad_img_kernel(half, *refs):
    row_place, col_place, scale_ref, logit_ref, txt_ref = refs[:5]
    rows_in, cols_in = refs[5:8], refs[8:12]
    grad_ref, dlogit_ref, *scalars = refs[12:-4]
    row_sum, col_sum, row_half, col_half = refs[-4:]
    step = pl.program_id(0)
    tile = logit_ref.shape[0]

    @pl.when(step == 0)
    def _():
        row_sum[...] = rows_in[0][...] + rows_in[1][...] + rows_in[2][...]
        col_sum[...] = cols_in[0][...] + cols_in[1][...] + cols_in[2][...] + cols_in[3][...]
        row = jnp.concatenate([row_sum[pl.ds(row_place[half * 8 + k], 1), 0:64] for k in range(8)], axis=1)
        col = jnp.concatenate([col_sum[pl.ds(col_place[k], 1), 0:64] for k in range(16)], axis=1)
        row_half[...] = jnp.broadcast_to(0.5 / row, (128, 512)).T
        col_half[...] = 0.5 / col
        lane = lax.broadcasted_iota(jnp.int32, (8, 128), 1)
        for out, sums, last in zip(scalars, (row_sum, col_sum), (row_sum[16:24, :], 0.0)):
            log_sum = jnp.sum(jnp.log(sums[0:16, 0:64]))
            slope = 0.5 * jnp.sum(sums[0:16, 64:128] / sums[0:16, 0:64])
            out[...] = jnp.where(lane == 0, log_sum, jnp.where(lane == 1, slope, last))

    start = pl.multiple_of(step * tile, tile)
    powers = jnp.exp(logit_ref[...] - scale_ref[1])
    by_row = jnp.concatenate([row_half[pl.ds(start, tile), :]] * 8, axis=1)
    dlogit = (powers * (by_row + col_half[...])).astype(BF16)
    dlogit_ref[...] = dlogit
    grad_ref[...] = jnp.dot(dlogit, txt_ref[...], preferred_element_type=F32).astype(BF16)


def grad_txt_kernel(low_ref, high_ref, img_ref, *grad_refs):
    step = pl.program_id(0)
    grad = sum(
        lax.dot_general(part[...], img_ref[k * 512 : (k + 1) * 512, :], (((0,), (0,)), ((), ())), preferred_element_type=F32)
        for k, part in enumerate((low_ref, high_ref))
    ).astype(BF16)
    for k, ref in enumerate(grad_refs):

        @pl.when(step == k)
        def _():
            ref[...] = grad


def finish_kernel(scale_ref, img_ref, txt_ref, img_hat_ref, txt_hat_ref, *refs):
    img_parts, txt_parts, (grad_img_ref, grad_txt_ref) = refs[:3], refs[3:7], refs[7:]
    for raw, other, parts, out in (
        (img_ref, txt_hat_ref, img_parts, grad_img_ref),
        (txt_ref, img_hat_ref, txt_parts, grad_txt_ref),
    ):
        values = raw[...].astype(F32)
        recip = 1.0 / jnp.sqrt(jnp.sum(values * values, axis=1, keepdims=True) + NORM_EPS)
        unit = values * recip
        total = sum(part[...].astype(F32) for part in parts)
        grad_hat = scale_ref[0] * (total - other[...].astype(F32))
        inner = jnp.sum(grad_hat * unit, axis=1, keepdims=True)
        out[...] = (recip * (grad_hat - unit * inner)).astype(BF16)


def places():
    y, z, core = lax.axis_index("y"), lax.axis_index("z"), lax.axis_index("c")
    x = 2 * lax.axis_index("xh") + lax.axis_index("xl")
    near = jnp.array([0, 3, 1, 2], jnp.int32)
    first, second = jnp.tile(near, 4), jnp.repeat(near, 4)
    on_x = jnp.where(core == 0, first, second)
    on_y = jnp.where(core == 0, second, first)
    cols = ((y + on_y) % 4) * 4 + (x + on_x) % 4
    distance = jnp.array([-1, -1, -2, -2, -3, -3, -4, 0, 1, 1, 2, 2, 3, 3, 4, 0], jnp.int32)
    others = jnp.array([1, 0, 1, 0, 1, 0, 1, 1, 0, 1, 0, 1, 0, 1, 0, 0], jnp.int32)
    way = jnp.where(core == 0, -1, 1)
    rows = ((core + others) % 2) * 8 + (z + way * distance) % 8
    return rows.astype(jnp.int32), cols.astype(jnp.int32)


def per_device(image_raw, text_raw, log_scale):
    rows, width = image_raw.shape
    total = rows * GROUP
    img_hat, txt_hat, diag = call(
        normalize_kernel,
        (shape(rows, width), shape(rows, width), shape(8, 128, dtype=F32)),
        [VMEM] * 2,
        "normalize",
    )(image_raw, text_raw)

    scale = jnp.exp(log_scale[0])
    shift = jnp.maximum(1.01 * scale - 70.0, 0.0)
    scales = jnp.stack([scale, shift])
    row_place, col_place = places()

    a1 = ring(img_hat, 1)
    sib = to_sibling(img_hat)
    b1 = ring(sib, 1)
    below, above, far = first_axis(txt_hat, 1), first_axis(txt_hat, -1), first_axis(txt_hat, 2)
    a2 = ring(a1, 1)
    b2 = ring(b1, 1)
    low = jnp.concatenate([txt_hat, below], axis=0)
    high = jnp.concatenate([above, far], axis=0)
    low_up, high_down = second_axis(low, 1), second_axis(high, -1)
    high_up, low_down = second_axis(high, 1), second_axis(low, -1)
    a3 = ring(a2, 1)
    b3 = ring(b2, 1)
    low_far, high_far = second_axis(low_up, 1), second_axis(high_down, -1)
    a4 = ring(a3, 1)
    mine = [a1, b1, a2, b2, a3, b3, a4]
    img_blocks = [to_sibling(block) for block in mine] + [sib] + mine + [img_hat]
    txt_blocks = [low, high, low_up, high_up, low_down, high_down, low_far, high_far]

    tile = 256
    steps = total // tile
    fixed = lambda *block: pl.BlockSpec(block, lambda i: (0,) * len(block))
    flops = 2 * total * total * width
    img_all, txt_all, logits, row_part, col_part = call(
        logits_kernel,
        (
            shape(total, width),
            shape(total, width),
            shape(total, total, dtype=F32),
            shape(24, 128, dtype=F32),
            shape(16, 128, dtype=F32),
        ),
        [SMEM] * 3 + [fixed(8, 128)] + [fixed(64, width)] * 16 + [fixed(128, width)] * 8,
        "logits",
        flops,
        grid=(steps,),
        out_specs=(
            fixed(total, width),
            fixed(total, width),
            pl.BlockSpec((total, tile), lambda i: (0, i)),
            fixed(24, 128),
            fixed(16, 128),
        ),
        scratch_shapes=[pltpu.VMEM((2, total, 128), F32)],
    )(row_place, col_place, scales, diag, *img_blocks, *txt_blocks)

    row_pair = row_part + to_sibling(row_part)
    col_line = col_part + along(col_part, "x", 1) + along(col_part, "x", 2) + along(col_part, "x", 3)
    lower, upper = along(row_pair, "z", 1), along(row_pair, "z", -1)
    two = row_pair + lower
    three = two + upper
    row_parts = [three, along(three, "z", 3), along(two, "z", -3)]
    col_parts = [col_line] + [along(col_line, "y", k) for k in (1, 2, 3)]

    def grad_img(half):
        scalars = (shape(8, 128, dtype=F32),) * 2 if half == 0 else ()
        return call(
            lambda *refs: grad_img_kernel(half, *refs),
            (shape(total // 2, width), shape(total // 2, total)) + scalars,
            [SMEM] * 3
            + [pl.BlockSpec((tile, total), lambda i: (i + half * steps // 2, 0)), fixed(total, width)]
            + [fixed(24, 128)] * 3
            + [fixed(16, 128)] * 4,
            f"grad_img{half}",
            flops // 2,
            grid=(steps // 2,),
            out_specs=(
                pl.BlockSpec((tile, width), lambda i: (i, 0)),
                pl.BlockSpec((tile, total), lambda i: (i, 0)),
            )
            + (fixed(8, 128),) * len(scalars),
            scratch_shapes=[
                pltpu.VMEM((24, 128), F32),
                pltpu.VMEM((16, 128), F32),
                pltpu.VMEM((total // 2, 128), F32),
                pltpu.VMEM((1, total), F32),
            ],
        )(row_place, col_place, scales, logits, txt_all, *row_parts, *col_parts)

    send, dlogits_low, row_scalars, col_scalars = grad_img(0)
    from_sibling = to_sibling(send)
    keep, dlogits_high = grad_img(1)
    txt_own, txt_minus, txt_plus, txt_far = call(
        grad_txt_kernel,
        (shape(256, width),) * 4,
        [pl.BlockSpec((total // 2, tile), lambda i: (0, i))] * 2 + [fixed(total, width)],
        "grad_txt",
        flops,
        grid=(steps,),
        out_specs=(fixed(256, width),) * 4,
    )(dlogits_low, dlogits_high, img_all)

    both = add(keep, from_sibling)
    blocks = [both[k * 64 : (k + 1) * 64] for k in range(8)]
    sum_a, sum_b = blocks[6], None
    sum_a = add(blocks[4], ring(sum_a, -1))
    sum_a, sum_b = add(blocks[2], ring(sum_a, -1)), add(blocks[3], ring(blocks[5], -1))
    sum_a, sum_b = add(blocks[0], ring(sum_a, -1)), add(blocks[1], ring(sum_b, -1))
    img_parts = [blocks[7], ring(sum_a, -1), to_sibling(ring(sum_b, -1))]

    to_minus = add(txt_minus[:128], second_axis(txt_far[:128], -1))
    to_plus = add(txt_plus[128:], second_axis(txt_far[128:], 1))
    line_low = add(txt_own[:128], second_axis(to_minus, -1), second_axis(txt_plus[:128], 1))
    line_high = add(txt_own[128:], second_axis(to_plus, 1), second_axis(txt_minus[128:], -1))
    txt_parts = [
        line_low[:64],
        first_axis(line_low[64:], -1),
        first_axis(line_high[:64], 1),
        first_axis(line_high[64:], 2),
    ]

    for axis, step in (("x", 1), ("x", 2), ("y", 1), ("y", 2)):
        row_scalars = row_scalars + swap(row_scalars, axis, step)
    for axis, step in (("c", 1), ("z", 1), ("z", 2), ("z", 4)):
        col_scalars = col_scalars + swap(col_scalars, axis, step)

    grad_image, grad_text = call(
        finish_kernel,
        (shape(rows, width),) * 2,
        [SMEM] + [VMEM] * 11,
        "finish",
    )(scales, image_raw, text_raw, img_hat, txt_hat, *img_parts, *txt_parts)

    batch = total * GROUP
    diag_sum = scale * row_scalars[0, 2]
    loss = (col_scalars[0, 0] + row_scalars[0, 0] + 2.0 * batch * shift - 2.0 * diag_sum) / (2 * batch)
    slope = (col_scalars[0, 1] + row_scalars[0, 1] - diag_sum) / batch
    return grad_image, grad_text, jnp.reshape(loss, (1,)), jnp.reshape(slope, (1,))


def swap(array, axis, bit):
    def move(x, y, z, c):
        return {
            "x": (x ^ bit, y, z, c),
            "y": (x, y ^ bit, z, c),
            "z": (x, y, z ^ bit, c),
            "c": (x, y, z, c ^ bit),
        }[axis]

    return permute(array, move)


def solution(mesh):
    mesh = Mesh(mesh.devices.reshape(SIZES), AXES)
    spec = P(AXES, None)
    return jax.shard_map(
        per_device, mesh=mesh, in_specs=(spec, spec, P()), out_specs=(spec, spec, P(), P()), check_vma=False
    )
```

```python
import itertools

import jax
import jax.numpy as jnp
from jax import lax
from jax.experimental import pallas as pl
from jax.experimental.pallas import tpu as pltpu
from jax.sharding import Mesh, PartitionSpec as P

NORM_EPS = 1e-06
AXES = ("y", "xh", "c", "xl", "z")
SIZES = (4, 2, 2, 2, 8)
GROUP = 16
ROWS = 64
VMEM_LIMIT = 24 * 1024 * 1024
F32 = jnp.float32
BF16 = jnp.bfloat16
VMEM = pl.BlockSpec(memory_space=pltpu.VMEM)
SMEM = pl.BlockSpec(memory_space=pltpu.SMEM)


def call(kernel, out, ins, name, flops=0, **more):
    return pl.pallas_call(
        kernel,
        out_shape=out,
        in_specs=ins,
        compiler_params=pltpu.CompilerParams(vmem_limit_bytes=VMEM_LIMIT),
        cost_estimate=pl.CostEstimate(flops=flops, bytes_accessed=1 << 20, transcendentals=0),
        name=name,
        **more,
    )


def shape(*dims, dtype=BF16):
    return jax.ShapeDtypeStruct(dims, dtype)


def permute(array, move):
    flat = lambda x, y, z, c: (((y * 2 + x // 2) * 2 + c) * 2 + x % 2) * 8 + z
    pairs = []
    for y, xh, c, xl, z in itertools.product(*map(range, SIZES)):
        x2, y2, z2, c2 = move(2 * xh + xl, y, z, c)
        pairs.append((flat(2 * xh + xl, y, z, c), flat(x2 % 4, y2 % 4, z2 % 8, c2 % 2)))
    return lax.ppermute(array, AXES, pairs)


def to_sibling(array):
    return permute(array, lambda x, y, z, c: (x, y, z, 1 - c))


def along(array, axis, step):
    steps = {"x": (step, 0, 0), "y": (0, step, 0), "z": (0, 0, step)}[axis]
    return permute(array, lambda x, y, z, c: (x + steps[0], y + steps[1], z + steps[2], c))


def first_axis(array, step):
    return permute(array, lambda x, y, z, c: (x + step, y, z, c) if c == 0 else (x, y + step, z, c))


def second_axis(array, step):
    return permute(array, lambda x, y, z, c: (x, y + step, z, c) if c == 0 else (x + step, y, z, c))


def ring(array, step):
    return permute(array, lambda x, y, z, c: (x, y, z + (step if c == 0 else -step), c))


def normalize_kernel(img_ref, txt_ref, img_hat_ref, txt_hat_ref, diag_ref):
    hats = []
    for raw, hat in ((img_ref, img_hat_ref), (txt_ref, txt_hat_ref)):
        values = raw[...].astype(F32)
        recip = 1.0 / jnp.sqrt(jnp.sum(values * values, axis=1, keepdims=True) + NORM_EPS)
        hat[...] = (values * recip).astype(BF16)
        hats.append(hat[...].astype(F32))
    diag_ref[...] = jnp.full(diag_ref.shape, jnp.sum(hats[0] * hats[1]), F32)


def encode(ref, at, scalars):
    high = scalars.astype(BF16).astype(F32)
    middle = (scalars - high).astype(BF16).astype(F32)
    parts = (high, middle, scalars - high - middle)
    row = lax.broadcasted_iota(jnp.int32, (16, 128), 0)
    block = jnp.zeros((16, 128), F32)
    for k, part in enumerate(parts):
        block = jnp.where(row == k, jnp.concatenate([part, part], axis=0), block)
    ref[at : at + 16, 0:128] = block.astype(BF16)
    ref[at : at + 16, 128:] = jnp.zeros((16, ref.shape[1] - 128), BF16)


def decode(ref, at):
    block = ref[at : at + 16, 0:128].astype(F32)
    return jnp.broadcast_to(jnp.sum(block, axis=0, keepdims=True), (8, 128))


def pair_kernel(core_ref, keep_ref, arrived_ref, far_ref, rest_ref, own_ref, scalar_ref):
    total = keep_ref[0:512, :].astype(F32) + arrived_ref[0:512, :].astype(F32)
    total = total.astype(BF16)
    rest_ref[...] = total[0:384]
    far_ref[0:64, :] = total[384:448]
    own_ref[...] = total[448:512]
    scalars = decode(keep_ref, 512) + decode(arrived_ref, 512)
    scalar_ref[...] = scalars
    encode(far_ref, 64, jnp.where(core_ref[0] == 0, scalars, 0.0))


def ring_fold_kernel(start, base_ref, arrived_ref, scalar_ref, out_ref):
    rows = arrived_ref.shape[0] - 16
    out_ref[0:rows, :] = (
        base_ref[start : start + rows, :].astype(F32) + arrived_ref[0:rows, :].astype(F32)
    ).astype(BF16)
    if rows < 128:
        out_ref[rows:128, :] = base_ref[start + rows : start + 128, :]
    encode(out_ref, 128, scalar_ref[...] + decode(arrived_ref, rows))


def plane_fold_kernel(minus_ref, plus_ref, low_ref, high_ref, scalar_ref, to_minus_ref, to_plus_ref):
    to_minus_ref[0:128, :] = (minus_ref[0:128, :].astype(F32) + low_ref[0:128, :].astype(F32)).astype(BF16)
    to_minus_ref[128:256, :] = minus_ref[128:256, :]
    to_plus_ref[0:128, :] = plus_ref[0:128, :]
    to_plus_ref[128:256, :] = (plus_ref[128:256, :].astype(F32) + high_ref[...].astype(F32)).astype(BF16)
    encode(to_minus_ref, 256, scalar_ref[...] + decode(low_ref, 128))
    encode(to_plus_ref, 256, scalar_ref[...])


def line_kernel(own_ref, down_ref, up_ref, scalar_ref, *outs):
    scalars = scalar_ref[...] + decode(down_ref, 256) + decode(up_ref, 256)
    for k, out in enumerate(outs[:4]):
        cut = slice(k * 64, (k + 1) * 64)
        out[0:64, :] = (
            own_ref[cut, :].astype(F32) + down_ref[cut, :].astype(F32) + up_ref[cut, :].astype(F32)
        ).astype(BF16)
        if k:
            encode(out, 64, scalars)
    outs[4][...] = scalars


def logits_kernel(counts, *refs):
    row_place, col_place, scale_ref, diag_ref = refs[:4]
    n_img, n_txt = len(counts[0]), len(counts[1])
    img_refs, txt_refs = refs[4 : 4 + n_img], refs[4 + n_img : 4 + n_img + n_txt]
    img_all, txt_all, logit_ref, row_ref, col_ref, row_acc = refs[4 + n_img + n_txt :]
    step = pl.program_id(0)
    tile = 256

    @pl.when(step == 0)
    def _():
        for blocks, sizes, target in ((img_refs, counts[0], img_all), (txt_refs, counts[1], txt_all)):
            at = 0
            for block, size in zip(blocks, sizes):
                target[at : at + size, :] = block[...]
                at += size
        row_acc[...] = jnp.zeros_like(row_acc)

    start = pl.multiple_of(step * tile, tile)
    block = txt_all[pl.ds(start, tile), :]
    logits = scale_ref[0] * lax.dot_general(
        img_all[...], block, (((1,), (1,)), ((), ())), preferred_element_type=F32
    )
    logit_ref[:, pl.ds(start, tile)] = logits
    powers = jnp.exp(logits - scale_ref[1])
    weighted = powers * logits
    for k in range(tile // 128):
        row_acc[0] += powers[:, k * 128 : (k + 1) * 128]
        row_acc[1] += weighted[:, k * 128 : (k + 1) * 128]
    sums = jnp.sum(powers, axis=0, keepdims=True)
    slopes = jnp.sum(weighted, axis=0, keepdims=True)
    for k in range(tile // 64):
        at = col_place[step * (tile // 64) + k]
        cut = slice(k * 64, (k + 1) * 64)
        col_ref[pl.ds(at, 1), :] = jnp.concatenate([sums[:, cut], slopes[:, cut]], axis=1)

    @pl.when(step == pl.num_programs(0) - 1)
    def _():
        sums = jnp.sum(row_acc[0].T, axis=0, keepdims=True)
        slopes = jnp.sum(row_acc[1].T, axis=0, keepdims=True)
        for k in range(GROUP):
            cut = slice(k * 64, (k + 1) * 64)
            row_ref[pl.ds(row_place[k], 1), :] = jnp.concatenate([sums[:, cut], slopes[:, cut]], axis=1)
        row_ref[16:24, :] = diag_ref[...]


def grad_img_kernel(half, *refs):
    row_place, col_place, scale_ref, logit_ref, txt_ref = refs[:5]
    rows_in, cols_in = refs[5:8], refs[8:12]
    grad_ref, dlogit_ref, *row_scalars = refs[12:-4]
    row_sum, col_sum, row_half, col_half = refs[-4:]
    step = pl.program_id(0)
    tile = 256

    @pl.when(step == 0)
    def _():
        row_sum[...] = rows_in[0][...] + rows_in[1][...] + rows_in[2][...]
        col_sum[...] = cols_in[0][...] + cols_in[1][...] + cols_in[2][...] + cols_in[3][...]
        row = jnp.concatenate([row_sum[pl.ds(row_place[half * 8 + k], 1), 0:64] for k in range(8)], axis=1)
        col = jnp.concatenate([col_sum[pl.ds(col_place[k], 1), 0:64] for k in range(16)], axis=1)
        row_half[...] = jnp.broadcast_to(0.5 / row, (128, 512)).T
        col_half[...] = 0.5 / col
        lane = lax.broadcasted_iota(jnp.int32, (8, 128), 1)

        def scalars(sums, last):
            log_sum = jnp.sum(jnp.log(sums[0:16, 0:64]))
            slope = 0.5 * jnp.sum(sums[0:16, 64:128] / sums[0:16, 0:64])
            return jnp.where(lane == 0, log_sum, jnp.where(lane == 1, slope, last))

        encode(grad_ref, 512, scalars(col_sum, 0.0))
        for out in row_scalars:
            out[...] = scalars(row_sum, row_sum[16:24, :])

    start = pl.multiple_of(step * tile, tile)
    powers = jnp.exp(logit_ref[pl.ds(half * 512 + start, tile), :] - scale_ref[1])
    by_row = jnp.concatenate([row_half[pl.ds(start, tile), :]] * 8, axis=1)
    dlogit = (powers * (by_row + col_half[...])).astype(BF16)
    dlogit_ref[pl.ds(start, tile), :] = dlogit
    grad_ref[pl.ds(start, tile), :] = jnp.dot(dlogit, txt_ref[...], preferred_element_type=F32).astype(BF16)


def grad_txt_kernel(low_ref, high_ref, img_ref, scalar_ref, *outs):
    step = pl.program_id(0)
    tile = 256
    start = pl.multiple_of(step * tile, tile)
    grad = sum(
        lax.dot_general(
            part[:, pl.ds(start, tile)],
            img_ref[k * 512 : (k + 1) * 512, :],
            (((0,), (0,)), ((), ())),
            preferred_element_type=F32,
        )
        for k, part in enumerate((low_ref, high_ref))
    ).astype(BF16)
    for k, ref in enumerate(outs[:3]):

        @pl.when(step == k)
        def _():
            ref[...] = grad

    @pl.when(step == 3)
    def _():
        outs[3][0:128, :] = grad[0:128]
        outs[4][...] = grad[128:256]
        encode(outs[3], 128, scalar_ref[...])


def finish_kernel(scale_ref, img_ref, txt_ref, img_hat_ref, txt_hat_ref, *refs):
    own_img, ring_img, sib_img, own_txt, txt1, txt2, txt3, col_ref, row_ref = refs[:9]
    grad_img_ref, grad_txt_ref, loss_ref, slope_ref = refs[9:]
    scale = scale_ref[0]
    for raw, other, parts, out in (
        (img_ref, txt_hat_ref, (own_img, ring_img, sib_img), grad_img_ref),
        (txt_ref, img_hat_ref, (own_txt, txt1, txt2, txt3), grad_txt_ref),
    ):
        values = raw[...].astype(F32)
        recip = 1.0 / jnp.sqrt(jnp.sum(values * values, axis=1, keepdims=True) + NORM_EPS)
        unit = values * recip
        total = sum(part[0:64, :].astype(F32) for part in parts)
        grad_hat = scale * (total - other[...].astype(F32))
        inner = jnp.sum(grad_hat * unit, axis=1, keepdims=True)
        out[...] = (recip * (grad_hat - unit * inner)).astype(BF16)
    cols = col_ref[...] + decode(ring_img, 128) + decode(sib_img, 64)
    rows = row_ref[...] + decode(txt1, 64) + decode(txt2, 64) + decode(txt3, 64)
    batch = ROWS * GROUP * GROUP
    diag_sum = scale * rows[0, 2]
    logs = cols[0, 0] + rows[0, 0] + 2.0 * batch * scale_ref[1]
    loss_ref[0] = (logs - 2.0 * diag_sum) / (2 * batch)
    slope_ref[0] = (cols[0, 1] + rows[0, 1] - diag_sum) / batch


def places():
    y, z, core = lax.axis_index("y"), lax.axis_index("z"), lax.axis_index("c")
    x = 2 * lax.axis_index("xh") + lax.axis_index("xl")
    near = jnp.array([0, 3, 1, 2], jnp.int32)
    first, second = jnp.tile(near, 4), jnp.repeat(near, 4)
    on_x = jnp.where(core == 0, first, second)
    on_y = jnp.where(core == 0, second, first)
    cols = ((y + on_y) % 4) * 4 + (x + on_x) % 4
    distance = jnp.array([-1, -1, -2, -2, -3, -3, -4, 0, 1, 1, 2, 2, 3, 3, 4, 0], jnp.int32)
    others = jnp.array([1, 0, 1, 0, 1, 0, 1, 1, 0, 1, 0, 1, 0, 1, 0, 0], jnp.int32)
    way = jnp.where(core == 0, -1, 1)
    rows = ((core + others) % 2) * 8 + (z + way * distance) % 8
    return rows.astype(jnp.int32), cols.astype(jnp.int32)


def per_device(image_raw, text_raw, log_scale):
    rows, width = image_raw.shape
    total = rows * GROUP
    img_hat, txt_hat, diag = call(
        normalize_kernel,
        (shape(rows, width), shape(rows, width), shape(8, 128, dtype=F32)),
        [VMEM] * 2,
        "normalize",
    )(image_raw, text_raw)

    scale = jnp.exp(log_scale[0])
    shift = jnp.maximum(1.01 * scale - 70.0, 0.0)
    scales = jnp.stack([scale, shift])
    row_place, col_place = places()

    below, above, far = first_axis(txt_hat, 1), first_axis(txt_hat, -1), first_axis(txt_hat, 2)
    sib = to_sibling(img_hat)
    chip = jnp.concatenate([img_hat, sib], axis=0)
    ring1 = ring(chip, 1)
    line = jnp.concatenate([txt_hat, below, above, far], axis=0)
    ring1, line = lax.optimization_barrier((ring1, line))
    up, down = second_axis(line, 1), second_axis(line, -1)
    ring2 = ring(ring1, 1)
    low_far, high_far = second_axis(up[:128], 1), second_axis(down[128:], -1)
    ring3 = ring(ring2, 1)
    ring4 = ring(ring3[:64], 1)
    mine = [ring1, ring2, ring3, ring4]
    img_blocks = [to_sibling(block) for block in mine] + [sib] + mine + [img_hat]
    txt_blocks = [line, up, down, low_far, high_far]
    counts = [[block.shape[0] for block in blocks] for blocks in (img_blocks, txt_blocks)]

    steps = total // 256
    flops = 2 * total * total * width
    img_all, txt_all, logits, row_part, col_part = call(
        lambda *refs: logits_kernel(counts, *refs),
        (
            shape(total, width),
            shape(total, width),
            shape(total, total, dtype=F32),
            shape(24, 128, dtype=F32),
            shape(16, 128, dtype=F32),
        ),
        [SMEM] * 3 + [VMEM] * (1 + len(img_blocks) + len(txt_blocks)),
        "logits",
        flops,
        grid=(steps,),
        out_specs=(VMEM,) * 5,
        scratch_shapes=[pltpu.VMEM((2, total, 128), F32)],
    )(row_place, col_place, scales, diag, *img_blocks, *txt_blocks)

    row_pair = row_part + to_sibling(row_part)
    col_line = col_part + along(col_part, "x", 1) + along(col_part, "x", 2) + along(col_part, "x", 3)
    lower, upper = along(row_pair, "z", 1), along(row_pair, "z", -1)
    two = row_pair + lower
    three = two + upper
    row_parts = [three, along(three, "z", 3), along(two, "z", -3)]
    col_parts = [col_line] + [along(col_line, "y", k) for k in (1, 2, 3)]

    def grad_img(half):
        row_scalars = (shape(8, 128, dtype=F32),) if half == 0 else ()
        return call(
            lambda *refs: grad_img_kernel(half, *refs),
            (shape(total // 2 + 16, width), shape(total // 2, total)) + row_scalars,
            [SMEM] * 3 + [VMEM] * 9,
            f"grad_img{half}",
            flops // 2,
            grid=(steps // 2,),
            out_specs=(VMEM,) * (2 + len(row_scalars)),
            scratch_shapes=[
                pltpu.VMEM((24, 128), F32),
                pltpu.VMEM((16, 128), F32),
                pltpu.VMEM((total // 2, 128), F32),
                pltpu.VMEM((1, total), F32),
            ],
        )(row_place, col_place, scales, logits, txt_all, *row_parts, *col_parts)

    core = jnp.reshape(lax.axis_index("c"), (1,)).astype(jnp.int32)
    send, dlogits_low, row_scalars = grad_img(0)
    arrived = to_sibling(send)
    keep, dlogits_high = grad_img(1)
    far, rest, own_img, col_scalars = call(
        pair_kernel,
        (shape(80, width), shape(384, width), shape(64, width), shape(8, 128, dtype=F32)),
        [SMEM] + [VMEM] * 2,
        "pair",
    )(core, keep, arrived)
    ring1 = ring(far, -1)
    txt_own, txt_minus, txt_plus, far_low, far_high = call(
        grad_txt_kernel,
        (shape(256, width),) * 3 + (shape(144, width), shape(128, width)),
        [VMEM] * 4,
        "grad_txt",
        flops,
        grid=(steps,),
        out_specs=(VMEM,) * 5,
    )(dlogits_low, dlogits_high, img_all, row_scalars)

    def ring_fold(start, arrived):
        return call(
            lambda *refs: ring_fold_kernel(start, *refs), shape(144, width), [VMEM] * 3, "ring_fold"
        )(rest, arrived, col_scalars)

    ring1, far_low, far_high = lax.optimization_barrier((ring1, far_low, far_high))
    low, high = second_axis(far_low, -1), second_axis(far_high, 1)
    ring2 = ring(ring_fold(256, ring1), -1)
    ring2, low, high = lax.optimization_barrier((ring2, low, high))
    to_minus, to_plus = call(
        plane_fold_kernel, (shape(272, width),) * 2, [VMEM] * 5, "plane_fold"
    )(txt_minus, txt_plus, low, high, row_scalars)
    down, up = second_axis(to_minus, -1), second_axis(to_plus, 1)
    ring3 = ring(ring_fold(128, ring2), -1)
    ring3, down, up = lax.optimization_barrier((ring3, down, up))
    own_txt, *sends, row_scalars = call(
        line_kernel,
        (shape(64, width),) + (shape(80, width),) * 3 + (shape(8, 128, dtype=F32),),
        [VMEM] * 4,
        "line",
    )(txt_own, down, up, row_scalars)
    ring4 = ring(ring_fold(0, ring3), -1)
    txt_parts = [own_txt] + [first_axis(part, step) for part, step in zip(sends, (-1, 1, 2))]
    img_parts = [own_img, ring4, to_sibling(ring4[64:])]

    scalar = shape(1, dtype=F32)
    return call(
        finish_kernel,
        (shape(rows, width), shape(rows, width), scalar, scalar),
        [SMEM] + [VMEM] * 13,
        "finish",
        out_specs=(VMEM, VMEM, SMEM, SMEM),
    )(scales, image_raw, text_raw, img_hat, txt_hat, *img_parts, *txt_parts, col_scalars, row_scalars)


def solution(mesh):
    mesh = Mesh(mesh.devices.reshape(SIZES), AXES)
    spec = P(AXES, None)
    return jax.shard_map(
        per_device, mesh=mesh, in_specs=(spec, spec, P()), out_specs=(spec, spec, P(), P()), check_vma=False
    )
```

```python
import itertools

import jax
import jax.numpy as jnp
from jax import lax
from jax.experimental import pallas as pl
from jax.experimental.pallas import tpu as pltpu
from jax.sharding import Mesh, PartitionSpec as P

NORM_EPS = 1e-06
AXES = ("y", "xh", "c", "xl", "z")
SIZES = (4, 2, 2, 2, 8)
GROUP = 16
ROWS = 64
VMEM_LIMIT = 24 * 1024 * 1024
F32 = jnp.float32
BF16 = jnp.bfloat16
VMEM = pl.BlockSpec(memory_space=pltpu.VMEM)
SMEM = pl.BlockSpec(memory_space=pltpu.SMEM)


def call(kernel, out, ins, name, flops=0, **more):
    return pl.pallas_call(
        kernel,
        out_shape=out,
        in_specs=ins,
        compiler_params=pltpu.CompilerParams(vmem_limit_bytes=VMEM_LIMIT),
        cost_estimate=pl.CostEstimate(flops=flops, bytes_accessed=1 << 20, transcendentals=0),
        name=name,
        **more,
    )


def shape(*dims, dtype=BF16):
    return jax.ShapeDtypeStruct(dims, dtype)


def permute(array, move):
    flat = lambda x, y, z, c: (((y * 2 + x // 2) * 2 + c) * 2 + x % 2) * 8 + z
    pairs = []
    for y, xh, c, xl, z in itertools.product(*map(range, SIZES)):
        x2, y2, z2, c2 = move(2 * xh + xl, y, z, c)
        pairs.append((flat(2 * xh + xl, y, z, c), flat(x2 % 4, y2 % 4, z2 % 8, c2 % 2)))
    return lax.ppermute(array, AXES, pairs)


def to_sibling(array):
    return permute(array, lambda x, y, z, c: (x, y, z, 1 - c))


def along(array, axis, step):
    steps = {"x": (step, 0, 0), "y": (0, step, 0), "z": (0, 0, step)}[axis]
    return permute(array, lambda x, y, z, c: (x + steps[0], y + steps[1], z + steps[2], c))


def first_axis(array, step):
    return permute(array, lambda x, y, z, c: (x + step, y, z, c) if c == 0 else (x, y + step, z, c))


def second_axis(array, step):
    return permute(array, lambda x, y, z, c: (x, y + step, z, c) if c == 0 else (x + step, y, z, c))


def ring(array, step):
    return permute(array, lambda x, y, z, c: (x, y, z + (step if c == 0 else -step), c))


def normalize_kernel(img_ref, txt_ref, img_hat_ref, txt_hat_ref, diag_ref):
    hats = []
    for raw, hat in ((img_ref, img_hat_ref), (txt_ref, txt_hat_ref)):
        values = raw[...].astype(F32)
        recip = 1.0 / jnp.sqrt(jnp.sum(values * values, axis=1, keepdims=True) + NORM_EPS)
        hat[...] = (values * recip).astype(BF16)
        hats.append(hat[...].astype(F32))
    diag_ref[...] = jnp.full(diag_ref.shape, jnp.sum(hats[0] * hats[1]), F32)


def encode(ref, at, scalars):
    high = scalars.astype(BF16).astype(F32)
    middle = (scalars - high).astype(BF16).astype(F32)
    parts = (high, middle, scalars - high - middle)
    row = lax.broadcasted_iota(jnp.int32, (16, 128), 0)
    block = jnp.zeros((16, 128), F32)
    for k, part in enumerate(parts):
        block = jnp.where(row == k, jnp.concatenate([part, part], axis=0), block)
    ref[at : at + 16, 0:128] = block.astype(BF16)
    ref[at : at + 16, 128:] = jnp.zeros((16, ref.shape[1] - 128), BF16)


def decode(ref, at):
    block = ref[at : at + 16, 0:128].astype(F32)
    return jnp.broadcast_to(jnp.sum(block, axis=0, keepdims=True), (8, 128))


def pair_kernel(core_ref, keep_ref, arrived_ref, far_ref, rest_ref, own_ref, scalar_ref):
    total = keep_ref[0:512, :].astype(F32) + arrived_ref[0:512, :].astype(F32)
    total = total.astype(BF16)
    rest_ref[...] = total[0:384]
    far_ref[0:64, :] = total[384:448]
    own_ref[...] = total[448:512]
    scalars = decode(keep_ref, 512) + decode(arrived_ref, 512)
    scalar_ref[...] = scalars
    encode(far_ref, 64, jnp.where(core_ref[0] == 0, scalars, 0.0))


def ring_fold_kernel(start, base_ref, arrived_ref, scalar_ref, out_ref):
    rows = arrived_ref.shape[0] - 16
    out_ref[0:rows, :] = (
        base_ref[start : start + rows, :].astype(F32) + arrived_ref[0:rows, :].astype(F32)
    ).astype(BF16)
    if rows < 128:
        out_ref[rows:128, :] = base_ref[start + rows : start + 128, :]
    encode(out_ref, 128, scalar_ref[...] + decode(arrived_ref, rows))


def last_fold_kernel(base_ref, arrived_ref, scalar_ref, own_ref, sib_ref):
    for k, out in enumerate((own_ref, sib_ref)):
        cut = slice(k * 64, (k + 1) * 64)
        out[0:64, :] = (base_ref[cut, :].astype(F32) + arrived_ref[cut, :].astype(F32)).astype(BF16)
    encode(sib_ref, 64, scalar_ref[...] + decode(arrived_ref, 128))


def plane_fold_kernel(minus_ref, plus_ref, low_ref, high_ref, scalar_ref, to_minus_ref, to_plus_ref):
    to_minus_ref[0:128, :] = (minus_ref[0:128, :].astype(F32) + low_ref[0:128, :].astype(F32)).astype(BF16)
    to_minus_ref[128:256, :] = minus_ref[128:256, :]
    to_plus_ref[0:128, :] = plus_ref[0:128, :]
    to_plus_ref[128:256, :] = (plus_ref[128:256, :].astype(F32) + high_ref[...].astype(F32)).astype(BF16)
    encode(to_minus_ref, 256, scalar_ref[...] + decode(low_ref, 128))
    encode(to_plus_ref, 256, scalar_ref[...])


def line_kernel(own_ref, down_ref, up_ref, scalar_ref, *outs):
    scalars = scalar_ref[...] + decode(down_ref, 256) + decode(up_ref, 256)
    for k, out in enumerate(outs[:4]):
        cut = slice(k * 64, (k + 1) * 64)
        out[0:64, :] = (
            own_ref[cut, :].astype(F32) + down_ref[cut, :].astype(F32) + up_ref[cut, :].astype(F32)
        ).astype(BF16)
        if k:
            encode(out, 64, scalars)
    outs[4][...] = scalars


def logits_kernel(img_order, txt_order, *refs):
    row_place, col_place, scale_ref, diag_ref = refs[:4]
    n_img, n_txt = 9, 5
    img_refs, txt_refs = refs[4 : 4 + n_img], refs[4 + n_img : 4 + n_img + n_txt]
    img_all, txt_all, logit_ref, row_ref, col_ref, row_acc = refs[4 + n_img + n_txt :]
    step = pl.program_id(0)
    tile = 256

    @pl.when(step == 0)
    def _():
        for blocks, order, target in ((img_refs, img_order, img_all), (txt_refs, txt_order, txt_all)):
            at = 0
            for k, first, size in order:
                target[at : at + size, :] = blocks[k][first : first + size, :]
                at += size
        row_acc[...] = jnp.zeros_like(row_acc)

    start = pl.multiple_of(step * tile, tile)
    block = txt_all[pl.ds(start, tile), :]
    logits = scale_ref[0] * lax.dot_general(
        img_all[...], block, (((1,), (1,)), ((), ())), preferred_element_type=F32
    )
    logit_ref[:, pl.ds(start, tile)] = logits
    powers = jnp.exp(logits - scale_ref[1])
    weighted = powers * logits
    for k in range(tile // 128):
        row_acc[0] += powers[:, k * 128 : (k + 1) * 128]
        row_acc[1] += weighted[:, k * 128 : (k + 1) * 128]
    sums = jnp.sum(powers, axis=0, keepdims=True)
    slopes = jnp.sum(weighted, axis=0, keepdims=True)
    for k in range(tile // 64):
        at = col_place[step * (tile // 64) + k]
        cut = slice(k * 64, (k + 1) * 64)
        col_ref[pl.ds(at, 1), :] = jnp.concatenate([sums[:, cut], slopes[:, cut]], axis=1)

    @pl.when(step == pl.num_programs(0) - 1)
    def _():
        sums = jnp.sum(row_acc[0].T, axis=0, keepdims=True)
        slopes = jnp.sum(row_acc[1].T, axis=0, keepdims=True)
        for k in range(GROUP):
            cut = slice(k * 64, (k + 1) * 64)
            row_ref[pl.ds(row_place[k], 1), :] = jnp.concatenate([sums[:, cut], slopes[:, cut]], axis=1)
        row_ref[16:24, :] = diag_ref[...]


def grad_img_kernel(half, *refs):
    row_place, col_place, scale_ref, logit_ref, txt_ref = refs[:5]
    rows_in, cols_in = refs[5:8], refs[8:12]
    grad_ref, dlogit_ref, *row_scalars = refs[12:-4]
    row_sum, col_sum, row_half, col_half = refs[-4:]
    step = pl.program_id(0)
    tile = 256

    @pl.when(step == 0)
    def _():
        row_sum[...] = rows_in[0][...] + rows_in[1][...] + rows_in[2][...]
        col_sum[...] = cols_in[0][...] + cols_in[1][...] + cols_in[2][...] + cols_in[3][...]
        row = jnp.concatenate([row_sum[pl.ds(row_place[half * 8 + k], 1), 0:64] for k in range(8)], axis=1)
        col = jnp.concatenate([col_sum[pl.ds(col_place[k], 1), 0:64] for k in range(16)], axis=1)
        row_half[...] = jnp.broadcast_to(0.5 / row, (128, 512)).T
        col_half[...] = 0.5 / col
        lane = lax.broadcasted_iota(jnp.int32, (8, 128), 1)

        def scalars(sums, last):
            log_sum = jnp.sum(jnp.log(sums[0:16, 0:64]))
            slope = 0.5 * jnp.sum(sums[0:16, 64:128] / sums[0:16, 0:64])
            return jnp.where(lane == 0, log_sum, jnp.where(lane == 1, slope, last))

        encode(grad_ref, 512, scalars(col_sum, 0.0))
        for out in row_scalars:
            out[...] = scalars(row_sum, row_sum[16:24, :])

    start = pl.multiple_of(step * tile, tile)
    powers = jnp.exp(logit_ref[pl.ds(half * 512 + start, tile), :] - scale_ref[1])
    by_row = jnp.concatenate([row_half[pl.ds(start, tile), :]] * 8, axis=1)
    dlogit = (powers * (by_row + col_half[...])).astype(BF16)
    dlogit_ref[pl.ds(start, tile), :] = dlogit
    grad_ref[pl.ds(start, tile), :] = jnp.dot(dlogit, txt_ref[...], preferred_element_type=F32).astype(BF16)


def grad_txt_tile(start, low_ref, high_ref, img_ref):
    return sum(
        lax.dot_general(
            part[:, pl.ds(start, 256)],
            img_ref[k * 512 : (k + 1) * 512, :],
            (((0,), (0,)), ((), ())),
            preferred_element_type=F32,
        )
        for k, part in enumerate((low_ref, high_ref))
    ).astype(BF16)


def grad_txt_far_kernel(low_ref, high_ref, img_ref, scalar_ref, far_low_ref, far_high_ref):
    grad = grad_txt_tile(768, low_ref, high_ref, img_ref)
    far_low_ref[0:128, :] = grad[0:128]
    far_high_ref[...] = grad[128:256]
    encode(far_low_ref, 128, scalar_ref[...])


def grad_txt_kernel(low_ref, high_ref, img_ref, *outs):
    step = pl.program_id(0)
    grad = grad_txt_tile(pl.multiple_of(step * 256, 256), low_ref, high_ref, img_ref)
    for k, ref in enumerate(outs):

        @pl.when(step == k)
        def _():
            ref[...] = grad


def finish_kernel(scale_ref, img_ref, txt_ref, img_hat_ref, txt_hat_ref, *refs):
    own_img, ring_img, sib_img, for_sib, own_txt, txt1, txt2, txt3, col_ref, row_ref = refs[:10]
    grad_img_ref, grad_txt_ref, loss_ref, slope_ref = refs[10:]
    scale = scale_ref[0]
    for raw, other, parts, out in (
        (img_ref, txt_hat_ref, (own_img, ring_img, sib_img), grad_img_ref),
        (txt_ref, img_hat_ref, (own_txt, txt1, txt2, txt3), grad_txt_ref),
    ):
        values = raw[...].astype(F32)
        recip = 1.0 / jnp.sqrt(jnp.sum(values * values, axis=1, keepdims=True) + NORM_EPS)
        unit = values * recip
        total = sum(part[0:64, :].astype(F32) for part in parts)
        grad_hat = scale * (total - other[...].astype(F32))
        inner = jnp.sum(grad_hat * unit, axis=1, keepdims=True)
        out[...] = (recip * (grad_hat - unit * inner)).astype(BF16)
    cols = col_ref[...] + decode(for_sib, 64) + decode(sib_img, 64)
    rows = row_ref[...] + decode(txt1, 64) + decode(txt2, 64) + decode(txt3, 64)
    batch = ROWS * GROUP * GROUP
    diag_sum = scale * rows[0, 2]
    logs = cols[0, 0] + rows[0, 0] + 2.0 * batch * scale_ref[1]
    loss_ref[0] = (logs - 2.0 * diag_sum) / (2 * batch)
    slope_ref[0] = (cols[0, 1] + rows[0, 1] - diag_sum) / batch


def places():
    y, z, core = lax.axis_index("y"), lax.axis_index("z"), lax.axis_index("c")
    x = 2 * lax.axis_index("xh") + lax.axis_index("xl")
    near = jnp.array([0, 3, 1, 2], jnp.int32)
    first, second = jnp.tile(near, 4), jnp.repeat(near, 4)
    on_x = jnp.where(core == 0, first, second)
    on_y = jnp.where(core == 0, second, first)
    cols = ((y + on_y) % 4) * 4 + (x + on_x) % 4
    distance = jnp.array([-1, -1, -2, -2, -3, -3, -4, 0, 1, 1, 2, 2, 3, 3, 4, 0], jnp.int32)
    others = jnp.array([1, 0, 1, 0, 1, 0, 1, 1, 0, 1, 0, 1, 0, 1, 0, 0], jnp.int32)
    way = jnp.where(core == 0, -1, 1)
    rows = ((core + others) % 2) * 8 + (z + way * distance) % 8
    return rows.astype(jnp.int32), cols.astype(jnp.int32)


def per_device(image_raw, text_raw, log_scale):
    rows, width = image_raw.shape
    total = rows * GROUP
    img_hat, txt_hat, diag = call(
        normalize_kernel,
        (shape(rows, width), shape(rows, width), shape(8, 128, dtype=F32)),
        [VMEM] * 2,
        "normalize",
    )(image_raw, text_raw)

    scale = jnp.exp(log_scale[0])
    shift = jnp.maximum(1.01 * scale - 70.0, 0.0)
    scales = jnp.stack([scale, shift])
    row_place, col_place = places()

    ring1_own = ring(img_hat, 1)
    sib = to_sibling(img_hat)
    below, above, far = first_axis(txt_hat, 1), first_axis(txt_hat, -1), first_axis(txt_hat, 2)
    ring1 = jnp.concatenate([ring1_own, ring(sib, 1)], axis=0)
    line = jnp.concatenate([txt_hat, below, above, far], axis=0)
    up, down = second_axis(line, 1), second_axis(line, -1)
    ring1, _ = lax.optimization_barrier((ring1, line))
    ring2 = ring(ring1, 1)
    low_far, high_far = second_axis(up[:128], 1), second_axis(down[128:], -1)
    ring3 = ring(ring2, 1)
    ring3, _, _ = lax.optimization_barrier((ring3, up, down))
    ring4 = ring(ring3, 1)
    img_blocks = [to_sibling(block) for block in (ring1, ring2, ring3)] + [sib, ring1, ring2, ring3, ring4, img_hat]
    img_order = [(0, 0, 128), (1, 0, 128), (2, 0, 128), (7, 64, 64), (3, 0, 64)]
    img_order += [(4, 0, 128), (5, 0, 128), (6, 0, 128), (7, 0, 64), (8, 0, 64)]
    txt_blocks = [line, up, down, low_far, high_far]
    txt_order = [(k, 0, block.shape[0]) for k, block in enumerate(txt_blocks)]

    steps = total // 256
    flops = 2 * total * total * width
    img_all, txt_all, logits, row_part, col_part = call(
        lambda *refs: logits_kernel(img_order, txt_order, *refs),
        (
            shape(total, width),
            shape(total, width),
            shape(total, total, dtype=F32),
            shape(24, 128, dtype=F32),
            shape(16, 128, dtype=F32),
        ),
        [SMEM] * 3 + [VMEM] * (1 + len(img_blocks) + len(txt_blocks)),
        "logits",
        flops,
        grid=(steps,),
        out_specs=(VMEM,) * 5,
        scratch_shapes=[pltpu.VMEM((2, total, 128), F32)],
    )(row_place, col_place, scales, diag, *img_blocks, *txt_blocks)

    row_pair = row_part + to_sibling(row_part)
    col_line = col_part + along(col_part, "x", 1) + along(col_part, "x", 2) + along(col_part, "x", 3)
    lower, upper = along(row_pair, "z", 1), along(row_pair, "z", -1)
    two = row_pair + lower
    three = two + upper
    row_parts = [three, along(three, "z", 3), along(two, "z", -3)]
    col_parts = [col_line] + [along(col_line, "y", k) for k in (1, 2, 3)]

    def grad_img(half):
        row_scalars = (shape(8, 128, dtype=F32),) if half == 0 else ()
        return call(
            lambda *refs: grad_img_kernel(half, *refs),
            (shape(total // 2 + 16, width), shape(total // 2, total)) + row_scalars,
            [SMEM] * 3 + [VMEM] * 9,
            f"grad_img{half}",
            flops // 2,
            grid=(steps // 2,),
            out_specs=(VMEM,) * (2 + len(row_scalars)),
            scratch_shapes=[
                pltpu.VMEM((24, 128), F32),
                pltpu.VMEM((16, 128), F32),
                pltpu.VMEM((total // 2, 128), F32),
                pltpu.VMEM((1, total), F32),
            ],
        )(row_place, col_place, scales, logits, txt_all, *row_parts, *col_parts)

    send, dlogits_low, row_scalars = grad_img(0)
    arrived = to_sibling(send)
    keep, dlogits_high = grad_img(1)
    core = jnp.reshape(lax.axis_index("c"), (1,)).astype(jnp.int32)
    far, rest, own_img, col_scalars = call(
        pair_kernel,
        (shape(80, width), shape(384, width), shape(64, width), shape(8, 128, dtype=F32)),
        [SMEM] + [VMEM] * 2,
        "pair",
    )(core, keep, arrived)
    ring1 = ring(far, -1)
    far_low, far_high = call(
        grad_txt_far_kernel,
        (shape(144, width), shape(128, width)),
        [VMEM] * 4,
        "grad_txt_far",
        flops // 4,
    )(dlogits_low, dlogits_high, img_all, row_scalars)
    low, high = second_axis(far_low, -1), second_axis(far_high, 1)
    txt_own, txt_minus, txt_plus = call(
        grad_txt_kernel,
        (shape(256, width),) * 3,
        [VMEM] * 3,
        "grad_txt",
        flops // 4 * 3,
        grid=(3,),
        out_specs=(VMEM,) * 3,
    )(dlogits_low, dlogits_high, img_all)

    def ring_fold(start, arrived):
        return call(
            lambda *refs: ring_fold_kernel(start, *refs), shape(144, width), [VMEM] * 3, "ring_fold"
        )(rest, arrived, col_scalars)

    ring1, _ = lax.optimization_barrier((ring1, txt_own))
    ring2 = ring(ring_fold(256, ring1), -1)
    to_minus, to_plus = call(
        plane_fold_kernel, (shape(272, width),) * 2, [VMEM] * 5, "plane_fold"
    )(txt_minus, txt_plus, low, high, row_scalars)
    down, up = second_axis(to_minus, -1), second_axis(to_plus, 1)
    ring2, _ = lax.optimization_barrier((ring2, to_plus))
    ring3 = ring(ring_fold(128, ring2), -1)
    own_txt, *sends, row_scalars = call(
        line_kernel,
        (shape(64, width),) + (shape(80, width),) * 3 + (shape(8, 128, dtype=F32),),
        [VMEM] * 4,
        "line",
    )(txt_own, down, up, row_scalars)
    ring3, _ = lax.optimization_barrier((ring3, own_txt))
    to_own, to_sib = call(
        last_fold_kernel, (shape(64, width), shape(80, width)), [VMEM] * 3, "last_fold"
    )(rest, ring3, col_scalars)
    for_sib = ring(to_sib, -1)
    txt_parts = [own_txt] + [first_axis(part, step) for part, step in zip(sends, (-1, 1, 2))]
    img_parts = [own_img, ring(to_own, -1), to_sibling(for_sib), for_sib]

    scalar = shape(1, dtype=F32)
    return call(
        finish_kernel,
        (shape(rows, width), shape(rows, width), scalar, scalar),
        [SMEM] + [VMEM] * 14,
        "finish",
        out_specs=(VMEM, VMEM, SMEM, SMEM),
    )(scales, image_raw, text_raw, img_hat, txt_hat, *img_parts, *txt_parts, col_scalars, row_scalars)


def solution(mesh):
    mesh = Mesh(mesh.devices.reshape(SIZES), AXES)
    spec = P(AXES, None)
    return jax.shard_map(
        per_device, mesh=mesh, in_specs=(spec, spec, P()), out_specs=(spec, spec, P(), P()), check_vma=False
    )
```

```python
import itertools

import jax
import jax.numpy as jnp
from jax import lax
from jax.experimental import pallas as pl
from jax.experimental.pallas import tpu as pltpu
from jax.sharding import Mesh, PartitionSpec as P

NORM_EPS = 1e-06
LOG2_E = 1.4426950408889634
AXES = ("y", "xh", "c", "xl", "z")
SIZES = (4, 2, 2, 2, 8)
GROUP = 16
ROWS = 64
VMEM_LIMIT = 24 * 1024 * 1024
F32 = jnp.float32
BF16 = jnp.bfloat16
VMEM = pl.BlockSpec(memory_space=pltpu.VMEM)
SMEM = pl.BlockSpec(memory_space=pltpu.SMEM)


def call(kernel, out, ins, name, flops=0, **more):
    return pl.pallas_call(
        kernel,
        out_shape=out,
        in_specs=ins,
        compiler_params=pltpu.CompilerParams(vmem_limit_bytes=VMEM_LIMIT),
        cost_estimate=pl.CostEstimate(flops=flops, bytes_accessed=1 << 20, transcendentals=0),
        name=name,
        **more,
    )


def shape(*dims, dtype=BF16):
    return jax.ShapeDtypeStruct(dims, dtype)


def permute(array, move):
    flat = lambda x, y, z, c: (((y * 2 + x // 2) * 2 + c) * 2 + x % 2) * 8 + z
    pairs = []
    for y, xh, c, xl, z in itertools.product(*map(range, SIZES)):
        x2, y2, z2, c2 = move(2 * xh + xl, y, z, c)
        pairs.append((flat(2 * xh + xl, y, z, c), flat(x2 % 4, y2 % 4, z2 % 8, c2 % 2)))
    return lax.ppermute(array, AXES, pairs)


def to_sibling(array):
    return permute(array, lambda x, y, z, c: (x, y, z, 1 - c))


def along(array, axis, step):
    steps = {"x": (step, 0, 0), "y": (0, step, 0), "z": (0, 0, step)}[axis]
    return permute(array, lambda x, y, z, c: (x + steps[0], y + steps[1], z + steps[2], c))


def first_axis(array, step):
    return permute(array, lambda x, y, z, c: (x + step, y, z, c) if c == 0 else (x, y + step, z, c))


def second_axis(array, step):
    return permute(array, lambda x, y, z, c: (x, y + step, z, c) if c == 0 else (x + step, y, z, c))


def ring(array, step):
    return permute(array, lambda x, y, z, c: (x, y, z + (step if c == 0 else -step), c))


def unit_rows(ref):
    values = ref[...].astype(F32)
    recip = 1.0 / jnp.sqrt(jnp.sum(values * values, axis=1, keepdims=True) + NORM_EPS)
    return values * recip, recip


def normalize_kernel(raw_ref, hat_ref):
    hat_ref[...] = unit_rows(raw_ref)[0].astype(BF16)


def diagonal_kernel(img_hat_ref, txt_hat_ref, diag_ref):
    products = img_hat_ref[...].astype(F32) * txt_hat_ref[...].astype(F32)
    diag_ref[...] = jnp.full(diag_ref.shape, jnp.sum(products), F32)


def encode(ref, at, scalars):
    high = scalars.astype(BF16).astype(F32)
    middle = (scalars - high).astype(BF16).astype(F32)
    parts = (high, middle, scalars - high - middle)
    row = lax.broadcasted_iota(jnp.int32, (16, 128), 0)
    block = jnp.zeros((16, 128), F32)
    for k, part in enumerate(parts):
        block = jnp.where(row == k, jnp.concatenate([part, part], axis=0), block)
    ref[at : at + 16, 0:128] = block.astype(BF16)
    ref[at : at + 16, 128:] = jnp.zeros((16, ref.shape[1] - 128), BF16)


def decode(ref, at):
    block = ref[at : at + 16, 0:128].astype(F32)
    return jnp.broadcast_to(jnp.sum(block, axis=0, keepdims=True), (8, 128))


def pair_kernel(core_ref, keep_ref, arrived_ref, far_ref, rest_ref, own_ref, scalar_ref):
    total = keep_ref[0:512, :].astype(F32) + arrived_ref[0:512, :].astype(F32)
    total = total.astype(BF16)
    rest_ref[...] = total[0:384]
    far_ref[0:64, :] = total[384:448]
    own_ref[...] = total[448:512]
    scalars = decode(keep_ref, 512) + decode(arrived_ref, 512)
    scalar_ref[...] = scalars
    encode(far_ref, 64, jnp.where(core_ref[0] == 0, scalars, 0.0))


def ring_fold_kernel(start, base_ref, arrived_ref, scalar_ref, out_ref):
    rows = arrived_ref.shape[0] - 16
    out_ref[0:rows, :] = (
        base_ref[start : start + rows, :].astype(F32) + arrived_ref[0:rows, :].astype(F32)
    ).astype(BF16)
    if rows < 128:
        out_ref[rows:128, :] = base_ref[start + rows : start + 128, :]
    encode(out_ref, 128, scalar_ref[...] + decode(arrived_ref, rows))


def last_fold_kernel(base_ref, arrived_ref, scalar_ref, own_ref, sib_ref):
    for k, out in enumerate((own_ref, sib_ref)):
        cut = slice(k * 64, (k + 1) * 64)
        out[0:64, :] = (base_ref[cut, :].astype(F32) + arrived_ref[cut, :].astype(F32)).astype(BF16)
    encode(sib_ref, 64, scalar_ref[...] + decode(arrived_ref, 128))


def plane_fold_kernel(minus_ref, plus_ref, low_ref, high_ref, scalar_ref, to_minus_ref, to_plus_ref):
    to_minus_ref[0:128, :] = (minus_ref[0:128, :].astype(F32) + low_ref[0:128, :].astype(F32)).astype(BF16)
    to_minus_ref[128:256, :] = minus_ref[128:256, :]
    to_plus_ref[0:128, :] = plus_ref[0:128, :]
    to_plus_ref[128:256, :] = (plus_ref[128:256, :].astype(F32) + high_ref[...].astype(F32)).astype(BF16)
    encode(to_minus_ref, 256, scalar_ref[...] + decode(low_ref, 128))
    encode(to_plus_ref, 256, scalar_ref[...])


def line_kernel(own_ref, down_ref, up_ref, scalar_ref, *outs):
    scalars = scalar_ref[...] + decode(down_ref, 256) + decode(up_ref, 256)
    for k, out in enumerate(outs[:4]):
        cut = slice(k * 64, (k + 1) * 64)
        out[0:64, :] = (
            own_ref[cut, :].astype(F32) + down_ref[cut, :].astype(F32) + up_ref[cut, :].astype(F32)
        ).astype(BF16)
        if k:
            encode(out, 64, scalars)
    outs[4][...] = scalars


def logits_kernel(img_order, txt_order, *refs):
    row_place, col_place, scale_ref, diag_ref = refs[:4]
    n_img, n_txt = 9, 5
    img_refs, txt_refs = refs[4 : 4 + n_img], refs[4 + n_img : 4 + n_img + n_txt]
    img_all, txt_all, logit_ref, row_ref, col_ref = refs[4 + n_img + n_txt :]
    tile = 256
    for blocks, order, target in ((img_refs, img_order, img_all), (txt_refs, txt_order, txt_all)):
        at = 0
        for k, first, size in order:
            target[at : at + size, :] = blocks[k][first : first + size, :]
            at += size
    row_sums, row_slopes = [], []
    for step in range(4):
        cut = slice(step * tile, (step + 1) * tile)
        logits = lax.dot_general(
            img_all[...], txt_all[cut, :], (((1,), (1,)), ((), ())), preferred_element_type=F32
        )
        logit_ref[:, cut] = logits
        powers = jnp.exp2(logits * scale_ref[2] - scale_ref[3])
        weighted = powers * logits
        row_sums.append(powers[:, 0:128] + powers[:, 128:256])
        row_slopes.append(weighted[:, 0:128] + weighted[:, 128:256])
        sums = jnp.sum(powers, axis=0, keepdims=True)
        slopes = jnp.sum(weighted, axis=0, keepdims=True)
        for k in range(tile // 64):
            at = col_place[step * (tile // 64) + k]
            part = slice(k * 64, (k + 1) * 64)
            col_ref[pl.ds(at, 1), :] = jnp.concatenate([sums[:, part], slopes[:, part]], axis=1)
    sums = jnp.sum(sum(row_sums).T, axis=0, keepdims=True)
    slopes = jnp.sum(sum(row_slopes).T, axis=0, keepdims=True)
    for k in range(GROUP):
        part = slice(k * 64, (k + 1) * 64)
        row_ref[pl.ds(row_place[k], 1), :] = jnp.concatenate([sums[:, part], slopes[:, part]], axis=1)
    row_ref[16:24, :] = diag_ref[...]


def grad_img_tiles(half, scale_ref, logit_ref, txt_ref, row_half, col_half, grad_ref, dlogit_ref):
    for step in range(2):
        cut = slice(step * 256, (step + 1) * 256)
        first = half * 512 + step * 256
        powers = jnp.exp2(logit_ref[first : first + 256, :] * scale_ref[2] - scale_ref[3])
        by_row = jnp.concatenate([row_half[first : first + 256, :]] * 8, axis=1)
        dlogit = (powers * (by_row + col_half[0:1, :])).astype(BF16)
        dlogit_ref[cut, :] = dlogit
        grad_ref[cut, :] = jnp.dot(dlogit, txt_ref[...], preferred_element_type=F32).astype(BF16)


def grad_img_kernel(*refs):
    row_place, col_place, scale_ref, logit_ref, txt_ref = refs[:5]
    rows_in, cols_in = refs[5:8], refs[8:12]
    grad_ref, dlogit_ref, row_half, col_half, row_scalars, col_scalars = refs[12:-2]
    row_sum, col_sum = refs[-2:]
    row_sum[...] = rows_in[0][...] + rows_in[1][...] + rows_in[2][...]
    col_sum[...] = cols_in[0][...] + cols_in[1][...] + cols_in[2][...] + cols_in[3][...]
    row = jnp.concatenate([row_sum[pl.ds(row_place[k], 1), 0:64] for k in range(16)], axis=1)
    col = jnp.concatenate([col_sum[pl.ds(col_place[k], 1), 0:64] for k in range(16)], axis=1)
    row_half[...] = jnp.broadcast_to(0.5 / row, (128, 1024)).T
    col_half[...] = jnp.broadcast_to(0.5 / col, (8, 1024))
    lane = lax.broadcasted_iota(jnp.int32, (8, 128), 1)

    def scalars(sums, last):
        log_sum = jnp.sum(jnp.log(sums[0:16, 0:64]))
        slope = 0.5 * jnp.sum(sums[0:16, 64:128] / sums[0:16, 0:64])
        return jnp.where(lane == 0, log_sum, jnp.where(lane == 1, slope, last))

    row_scalars[...] = scalars(row_sum, row_sum[16:24, :])
    col_scalars[...] = scalars(col_sum, 0.0)
    encode(grad_ref, 512, col_scalars[...])
    grad_img_tiles(0, scale_ref, logit_ref, txt_ref, row_half, col_half, grad_ref, dlogit_ref)


def grad_img_rest_kernel(scale_ref, logit_ref, txt_ref, row_half, col_half, scalar_ref, grad_ref, dlogit_ref):
    encode(grad_ref, 512, scalar_ref[...])
    grad_img_tiles(1, scale_ref, logit_ref, txt_ref, row_half, col_half, grad_ref, dlogit_ref)


def grad_txt_tile(start, low_ref, high_ref, img_ref):
    return sum(
        lax.dot_general(
            part[:, pl.ds(start, 256)],
            img_ref[k * 512 : (k + 1) * 512, :],
            (((0,), (0,)), ((), ())),
            preferred_element_type=F32,
        )
        for k, part in enumerate((low_ref, high_ref))
    ).astype(BF16)


def grad_txt_far_kernel(low_ref, high_ref, img_ref, scalar_ref, far_low_ref, far_high_ref):
    grad = grad_txt_tile(768, low_ref, high_ref, img_ref)
    far_low_ref[0:128, :] = grad[0:128]
    far_high_ref[...] = grad[128:256]
    encode(far_low_ref, 128, scalar_ref[...])


def grad_txt_kernel(low_ref, high_ref, img_ref, *outs):
    step = pl.program_id(0)
    grad = grad_txt_tile(pl.multiple_of(step * 256, 256), low_ref, high_ref, img_ref)
    for k, ref in enumerate(outs):

        @pl.when(step == k)
        def _():
            ref[...] = grad


def finish_kernel(scale_ref, img_ref, txt_ref, img_hat_ref, txt_hat_ref, *refs):
    own_img, ring_img, sib_img, for_sib, own_txt, txt1, txt2, txt3, col_ref, row_ref = refs[:10]
    grad_img_ref, grad_txt_ref, loss_ref, slope_ref = refs[10:]
    scale = scale_ref[0]
    for raw, other, parts, out in (
        (img_ref, txt_hat_ref, (own_img, ring_img, sib_img), grad_img_ref),
        (txt_ref, img_hat_ref, (own_txt, txt1, txt2, txt3), grad_txt_ref),
    ):
        unit, recip = unit_rows(raw)
        total = sum(part[0:64, :].astype(F32) for part in parts)
        grad_hat = scale * (total - other[...].astype(F32))
        inner = jnp.sum(grad_hat * unit, axis=1, keepdims=True)
        out[...] = (recip * (grad_hat - unit * inner)).astype(BF16)
    cols = col_ref[...] + decode(for_sib, 64) + decode(sib_img, 64)
    rows = row_ref[...] + decode(txt1, 64) + decode(txt2, 64) + decode(txt3, 64)
    batch = ROWS * GROUP * GROUP
    diag_sum = scale * rows[0, 2]
    logs = cols[0, 0] + rows[0, 0] + 2.0 * batch * scale_ref[1]
    loss_ref[0] = (logs - 2.0 * diag_sum) / (2 * batch)
    slope_ref[0] = (scale * (cols[0, 1] + rows[0, 1]) - diag_sum) / batch


def places():
    y, z, core = lax.axis_index("y"), lax.axis_index("z"), lax.axis_index("c")
    x = 2 * lax.axis_index("xh") + lax.axis_index("xl")
    near = jnp.array([0, 3, 1, 2], jnp.int32)
    first, second = jnp.tile(near, 4), jnp.repeat(near, 4)
    on_x = jnp.where(core == 0, first, second)
    on_y = jnp.where(core == 0, second, first)
    cols = ((y + on_y) % 4) * 4 + (x + on_x) % 4
    distance = jnp.array([-1, -1, -2, -2, -3, -3, -4, 0, 1, 1, 2, 2, 3, 3, 4, 0], jnp.int32)
    others = jnp.array([1, 0, 1, 0, 1, 0, 1, 1, 0, 1, 0, 1, 0, 1, 0, 0], jnp.int32)
    way = jnp.where(core == 0, -1, 1)
    rows = ((core + others) % 2) * 8 + (z + way * distance) % 8
    return rows.astype(jnp.int32), cols.astype(jnp.int32)


def per_device(image_raw, text_raw, log_scale):
    rows, width = image_raw.shape
    total = rows * GROUP
    img_hat = call(normalize_kernel, shape(rows, width), [VMEM], "normalize_img")(image_raw)
    txt_hat = call(normalize_kernel, shape(rows, width), [VMEM], "normalize_txt")(text_raw)
    diag = call(diagonal_kernel, shape(8, 128, dtype=F32), [VMEM] * 2, "diagonal")(img_hat, txt_hat)

    scale = jnp.exp(log_scale[0])
    shift = jnp.maximum(1.01 * scale - 70.0, 0.0)
    scales = jnp.stack([scale, shift, scale * LOG2_E, shift * LOG2_E])
    row_place, col_place = places()

    ring1_own = ring(img_hat, 1)
    sib = to_sibling(img_hat)
    below, above, far = first_axis(txt_hat, 1), first_axis(txt_hat, -1), first_axis(txt_hat, 2)
    ring1 = jnp.concatenate([ring1_own, ring(sib, 1)], axis=0)
    line = jnp.concatenate([txt_hat, below, above, far], axis=0)
    up, down = second_axis(line, 1), second_axis(line, -1)
    ring1, _ = lax.optimization_barrier((ring1, line))
    ring2 = ring(ring1, 1)
    low_far, high_far = second_axis(up[:128], 1), second_axis(down[128:], -1)
    ring3 = ring(ring2, 1)
    ring3, _, _ = lax.optimization_barrier((ring3, up, down))
    ring4 = ring(ring3, 1)
    img_blocks = [to_sibling(block) for block in (ring1, ring2, ring3)] + [sib, ring1, ring2, ring3, ring4, img_hat]
    img_order = [(0, 0, 128), (1, 0, 128), (2, 0, 128), (7, 64, 64), (3, 0, 64)]
    img_order += [(4, 0, 128), (5, 0, 128), (6, 0, 128), (7, 0, 64), (8, 0, 64)]
    txt_blocks = [line, up, down, low_far, high_far]
    txt_order = [(k, 0, block.shape[0]) for k, block in enumerate(txt_blocks)]

    flops = 2 * total * total * width
    img_all, txt_all, logits, row_part, col_part = call(
        lambda *refs: logits_kernel(img_order, txt_order, *refs),
        (
            shape(total, width),
            shape(total, width),
            shape(total, total, dtype=F32),
            shape(24, 128, dtype=F32),
            shape(16, 128, dtype=F32),
        ),
        [SMEM] * 3 + [VMEM] * (1 + len(img_blocks) + len(txt_blocks)),
        "logits",
        flops,
    )(row_place, col_place, scales, diag, *img_blocks, *txt_blocks)

    row_pair = row_part + to_sibling(row_part)
    col_line = col_part + along(col_part, "x", 1) + along(col_part, "x", 2) + along(col_part, "x", 3)
    lower, upper = along(row_pair, "z", 1), along(row_pair, "z", -1)
    two = row_pair + lower
    three = two + upper
    row_parts = [three, along(three, "z", 3), along(two, "z", -3)]
    col_parts = [col_line] + [along(col_line, "y", k) for k in (1, 2, 3)]

    eight = shape(8, 128, dtype=F32)
    half_grad = (shape(total // 2 + 16, width), shape(total // 2, total))
    send, dlogits_low, row_half, col_half, row_scalars, col_scalars = call(
        grad_img_kernel,
        half_grad + (shape(total, 128, dtype=F32), shape(8, total, dtype=F32), eight, eight),
        [SMEM] * 3 + [VMEM] * 9,
        "grad_img",
        flops // 2,
        scratch_shapes=[pltpu.VMEM((24, 128), F32), pltpu.VMEM((16, 128), F32)],
    )(row_place, col_place, scales, logits, txt_all, *row_parts, *col_parts)
    arrived = to_sibling(send)
    keep, dlogits_high = call(
        grad_img_rest_kernel,
        half_grad,
        [SMEM] + [VMEM] * 5,
        "grad_img_rest",
        flops // 2,
    )(scales, logits, txt_all, row_half, col_half, col_scalars)
    core = jnp.reshape(lax.axis_index("c"), (1,)).astype(jnp.int32)
    far, rest, own_img, col_scalars = call(
        pair_kernel,
        (shape(80, width), shape(384, width), shape(64, width), shape(8, 128, dtype=F32)),
        [SMEM] + [VMEM] * 2,
        "pair",
    )(core, keep, arrived)
    ring1 = ring(far, -1)
    far_low, far_high = call(
        grad_txt_far_kernel,
        (shape(144, width), shape(128, width)),
        [VMEM] * 4,
        "grad_txt_far",
        flops // 4,
    )(dlogits_low, dlogits_high, img_all, row_scalars)
    low, high = second_axis(far_low, -1), second_axis(far_high, 1)
    txt_own, txt_minus, txt_plus = call(
        grad_txt_kernel,
        (shape(256, width),) * 3,
        [VMEM] * 3,
        "grad_txt",
        flops // 4 * 3,
        grid=(3,),
        out_specs=(VMEM,) * 3,
    )(dlogits_low, dlogits_high, img_all)

    def ring_fold(start, arrived):
        return call(
            lambda *refs: ring_fold_kernel(start, *refs), shape(144, width), [VMEM] * 3, "ring_fold"
        )(rest, arrived, col_scalars)

    ring1, _ = lax.optimization_barrier((ring1, txt_own))
    ring2 = ring(ring_fold(256, ring1), -1)
    to_minus, to_plus = call(
        plane_fold_kernel, (shape(272, width),) * 2, [VMEM] * 5, "plane_fold"
    )(txt_minus, txt_plus, low, high, row_scalars)
    down, up = second_axis(to_minus, -1), second_axis(to_plus, 1)
    ring2, _ = lax.optimization_barrier((ring2, to_plus))
    ring3 = ring(ring_fold(128, ring2), -1)
    own_txt, *sends, row_scalars = call(
        line_kernel,
        (shape(64, width),) + (shape(80, width),) * 3 + (shape(8, 128, dtype=F32),),
        [VMEM] * 4,
        "line",
    )(txt_own, down, up, row_scalars)
    to_own, to_sib = call(
        last_fold_kernel, (shape(64, width), shape(80, width)), [VMEM] * 3, "last_fold"
    )(rest, ring3, col_scalars)
    for_sib = ring(to_sib, -1)
    txt_parts = [own_txt] + [first_axis(part, step) for part, step in zip(sends, (-1, 1, 2))]
    img_parts = [own_img, ring(to_own, -1), to_sibling(for_sib), for_sib]

    scalar = shape(1, dtype=F32)
    return call(
        finish_kernel,
        (shape(rows, width), shape(rows, width), scalar, scalar),
        [SMEM] + [VMEM] * 14,
        "finish",
        out_specs=(VMEM, VMEM, SMEM, SMEM),
    )(scales, image_raw, text_raw, img_hat, txt_hat, *img_parts, *txt_parts, col_scalars, row_scalars)


def solution(mesh):
    mesh = Mesh(mesh.devices.reshape(SIZES), AXES)
    spec = P(AXES, None)
    return jax.shard_map(
        per_device, mesh=mesh, in_specs=(spec, spec, P()), out_specs=(spec, spec, P(), P()), check_vma=False
    )
```

```python
import itertools

import jax
import jax.numpy as jnp
from jax import lax
from jax.experimental import pallas as pl
from jax.experimental.pallas import tpu as pltpu
from jax.sharding import Mesh, PartitionSpec as P

NORM_EPS = 1e-06
LOG2_E = 1.4426950408889634
AXES = ("y", "xh", "c", "xl", "z")
SIZES = (4, 2, 2, 2, 8)
GROUP = 16
ROWS = 64
VMEM_LIMIT = 24 * 1024 * 1024
F32 = jnp.float32
BF16 = jnp.bfloat16
VMEM = pl.BlockSpec(memory_space=pltpu.VMEM)
SMEM = pl.BlockSpec(memory_space=pltpu.SMEM)


def call(kernel, out, ins, name, flops=0, **more):
    return pl.pallas_call(
        kernel,
        out_shape=out,
        in_specs=ins,
        compiler_params=pltpu.CompilerParams(vmem_limit_bytes=VMEM_LIMIT),
        cost_estimate=pl.CostEstimate(flops=flops, bytes_accessed=1 << 20, transcendentals=0),
        name=name,
        **more,
    )


def shape(*dims, dtype=BF16):
    return jax.ShapeDtypeStruct(dims, dtype)


def permute(array, move):
    flat = lambda x, y, z, c: (((y * 2 + x // 2) * 2 + c) * 2 + x % 2) * 8 + z
    pairs = []
    for y, xh, c, xl, z in itertools.product(*map(range, SIZES)):
        x2, y2, z2, c2 = move(2 * xh + xl, y, z, c)
        pairs.append((flat(2 * xh + xl, y, z, c), flat(x2 % 4, y2 % 4, z2 % 8, c2 % 2)))
    return lax.ppermute(array, AXES, pairs)


def to_sibling(array):
    return permute(array, lambda x, y, z, c: (x, y, z, 1 - c))


def along(array, axis, step):
    steps = {"x": (step, 0, 0), "y": (0, step, 0), "z": (0, 0, step)}[axis]
    return permute(array, lambda x, y, z, c: (x + steps[0], y + steps[1], z + steps[2], c))


def first_axis(array, step):
    return permute(array, lambda x, y, z, c: (x + step, y, z, c) if c == 0 else (x, y + step, z, c))


def second_axis(array, step):
    return permute(array, lambda x, y, z, c: (x, y + step, z, c) if c == 0 else (x + step, y, z, c))


def ring(array, step):
    return permute(array, lambda x, y, z, c: (x, y, z + (step if c == 0 else -step), c))


def unit_rows(ref):
    values = ref[...].astype(F32)
    recip = 1.0 / jnp.sqrt(jnp.sum(values * values, axis=1, keepdims=True) + NORM_EPS)
    return values * recip, recip


def normalize_kernel(raw_ref, hat_ref):
    hat_ref[...] = unit_rows(raw_ref)[0].astype(BF16)


def diagonal_kernel(img_hat_ref, txt_hat_ref, diag_ref):
    products = img_hat_ref[...].astype(F32) * txt_hat_ref[...].astype(F32)
    diag_ref[...] = jnp.full(diag_ref.shape, jnp.sum(products), F32)


def encode(ref, at, scalars):
    high = scalars.astype(BF16).astype(F32)
    middle = (scalars - high).astype(BF16).astype(F32)
    parts = (high, middle, scalars - high - middle)
    row = lax.broadcasted_iota(jnp.int32, (16, 128), 0)
    block = jnp.zeros((16, 128), F32)
    for k, part in enumerate(parts):
        block = jnp.where(row == k, jnp.concatenate([part, part], axis=0), block)
    ref[at : at + 16, 0:128] = block.astype(BF16)
    ref[at : at + 16, 128:] = jnp.zeros((16, ref.shape[1] - 128), BF16)


def decode(ref, at):
    block = ref[at : at + 16, 0:128].astype(F32)
    return jnp.broadcast_to(jnp.sum(block, axis=0, keepdims=True), (8, 128))


def pair_kernel(core_ref, keep_ref, arrived_ref, far_ref, rest_ref, own_ref, scalar_ref):
    total = keep_ref[0:512, :].astype(F32) + arrived_ref[0:512, :].astype(F32)
    total = total.astype(BF16)
    rest_ref[...] = total[0:384]
    far_ref[0:64, :] = total[384:448]
    own_ref[...] = total[448:512]
    scalars = decode(keep_ref, 512) + decode(arrived_ref, 512)
    scalar_ref[...] = scalars
    encode(far_ref, 64, jnp.where(core_ref[0] == 0, scalars, 0.0))


def ring_fold_kernel(start, base_ref, arrived_ref, scalar_ref, out_ref):
    rows = arrived_ref.shape[0] - 16
    out_ref[0:rows, :] = (
        base_ref[start : start + rows, :].astype(F32) + arrived_ref[0:rows, :].astype(F32)
    ).astype(BF16)
    if rows < 128:
        out_ref[rows:128, :] = base_ref[start + rows : start + 128, :]
    encode(out_ref, 128, scalar_ref[...] + decode(arrived_ref, rows))


def last_fold_kernel(base_ref, arrived_ref, scalar_ref, own_ref, sib_ref):
    for k, out in enumerate((own_ref, sib_ref)):
        cut = slice(k * 64, (k + 1) * 64)
        out[0:64, :] = (base_ref[cut, :].astype(F32) + arrived_ref[cut, :].astype(F32)).astype(BF16)
    encode(sib_ref, 64, scalar_ref[...] + decode(arrived_ref, 128))


def plane_fold_kernel(minus_ref, plus_ref, low_ref, high_ref, scalar_ref, to_minus_ref, to_plus_ref):
    to_minus_ref[0:128, :] = (minus_ref[0:128, :].astype(F32) + low_ref[0:128, :].astype(F32)).astype(BF16)
    to_minus_ref[128:256, :] = minus_ref[128:256, :]
    to_plus_ref[0:128, :] = plus_ref[0:128, :]
    to_plus_ref[128:256, :] = (plus_ref[128:256, :].astype(F32) + high_ref[...].astype(F32)).astype(BF16)
    encode(to_minus_ref, 256, scalar_ref[...] + decode(low_ref, 128))
    encode(to_plus_ref, 256, scalar_ref[...])


def line_kernel(own_ref, down_ref, up_ref, scalar_ref, *outs):
    scalars = scalar_ref[...] + decode(down_ref, 256) + decode(up_ref, 256)
    for k, out in enumerate(outs[:4]):
        cut = slice(k * 64, (k + 1) * 64)
        out[0:64, :] = (
            own_ref[cut, :].astype(F32) + down_ref[cut, :].astype(F32) + up_ref[cut, :].astype(F32)
        ).astype(BF16)
        if k:
            encode(out, 64, scalars)
    outs[4][...] = scalars


def copy_rows(source, first, target, at, rows):
    @pl.loop(0, rows // 32)
    def _(k):
        cut = pl.ds(pl.multiple_of(first + k * 32, 32), 32)
        target[pl.ds(pl.multiple_of(at + k * 32, 32), 32), :] = source[cut, :]


def logits_kernel(img_order, txt_order, *refs):
    row_place, col_place, scale_ref, diag_ref = refs[:4]
    n_img, n_txt = 9, 5
    img_refs, txt_refs = refs[4 : 4 + n_img], refs[4 + n_img : 4 + n_img + n_txt]
    img_all, txt_all, logit_ref, row_ref, col_ref = refs[4 + n_img + n_txt :]
    tile = 256
    for blocks, order, target in ((img_refs, img_order, img_all), (txt_refs, txt_order, txt_all)):
        at = 0
        for k, first, size in order:
            copy_rows(blocks[k], first, target, at, size)
            at += size
    row_sums, row_slopes = [], []
    for step in range(4):
        cut = slice(step * tile, (step + 1) * tile)
        logits = lax.dot_general(
            img_all[...], txt_all[cut, :], (((1,), (1,)), ((), ())), preferred_element_type=F32
        )
        logit_ref[:, cut] = logits
        powers = jnp.exp2(logits * scale_ref[2] - scale_ref[3])
        weighted = powers * logits
        row_sums.append(powers[:, 0:128] + powers[:, 128:256])
        row_slopes.append(weighted[:, 0:128] + weighted[:, 128:256])
        sums = jnp.sum(powers, axis=0, keepdims=True)
        slopes = jnp.sum(weighted, axis=0, keepdims=True)
        for k in range(tile // 64):
            at = col_place[step * (tile // 64) + k]
            part = slice(k * 64, (k + 1) * 64)
            col_ref[pl.ds(at, 1), :] = jnp.concatenate([sums[:, part], slopes[:, part]], axis=1)
    sums = jnp.sum(sum(row_sums).T, axis=0, keepdims=True)
    slopes = jnp.sum(sum(row_slopes).T, axis=0, keepdims=True)
    for k in range(GROUP):
        part = slice(k * 64, (k + 1) * 64)
        row_ref[pl.ds(row_place[k], 1), :] = jnp.concatenate([sums[:, part], slopes[:, part]], axis=1)
    row_ref[16:24, :] = diag_ref[...]


def grad_img_tiles(half, scale_ref, logit_ref, txt_ref, row_half, col_half, grad_ref, dlogit_ref):
    rows = slice(half * 512, (half + 1) * 512)
    powers = jnp.exp2(logit_ref[rows, :] * scale_ref[2] - scale_ref[3])
    by_row = jnp.concatenate([row_half[rows, :]] * 8, axis=1)
    dlogit_ref[...] = (powers * (by_row + col_half[0:1, :])).astype(BF16)

    @pl.loop(0, 5)
    def _(step):
        cut = pl.ds(pl.multiple_of(step * 256, 256), 256)
        grad = jnp.dot(dlogit_ref[...], txt_ref[:, cut], preferred_element_type=F32)
        grad_ref[0:512, cut] = grad.astype(BF16)


def grad_img_kernel(*refs):
    row_place, col_place, scale_ref, logit_ref, txt_ref = refs[:5]
    rows_in, cols_in = refs[5:8], refs[8:12]
    grad_ref, dlogit_ref, row_half, col_half, row_scalars, col_scalars = refs[12:-2]
    row_sum, col_sum = refs[-2:]
    row_sum[...] = rows_in[0][...] + rows_in[1][...] + rows_in[2][...]
    col_sum[...] = cols_in[0][...] + cols_in[1][...] + cols_in[2][...] + cols_in[3][...]
    row = jnp.concatenate([row_sum[pl.ds(row_place[k], 1), 0:64] for k in range(16)], axis=1)
    col = jnp.concatenate([col_sum[pl.ds(col_place[k], 1), 0:64] for k in range(16)], axis=1)
    row_half[...] = jnp.broadcast_to(0.5 / row, (128, 1024)).T
    col_half[...] = jnp.broadcast_to(0.5 / col, (8, 1024))
    lane = lax.broadcasted_iota(jnp.int32, (8, 128), 1)

    def scalars(sums, last):
        log_sum = jnp.sum(jnp.log(sums[0:16, 0:64]))
        slope = 0.5 * jnp.sum(sums[0:16, 64:128] / sums[0:16, 0:64])
        return jnp.where(lane == 0, log_sum, jnp.where(lane == 1, slope, last))

    row_scalars[...] = scalars(row_sum, row_sum[16:24, :])
    col_scalars[...] = scalars(col_sum, 0.0)
    encode(grad_ref, 512, col_scalars[...])
    grad_img_tiles(0, scale_ref, logit_ref, txt_ref, row_half, col_half, grad_ref, dlogit_ref)


def grad_img_rest_kernel(scale_ref, logit_ref, txt_ref, row_half, col_half, scalar_ref, grad_ref, dlogit_ref):
    encode(grad_ref, 512, scalar_ref[...])
    grad_img_tiles(1, scale_ref, logit_ref, txt_ref, row_half, col_half, grad_ref, dlogit_ref)


def grad_txt_tile(start, low_ref, high_ref, img_ref):
    return sum(
        lax.dot_general(
            part[:, pl.ds(start, 256)],
            img_ref[k * 512 : (k + 1) * 512, :],
            (((0,), (0,)), ((), ())),
            preferred_element_type=F32,
        )
        for k, part in enumerate((low_ref, high_ref))
    ).astype(BF16)


def grad_txt_far_kernel(low_ref, high_ref, img_ref, scalar_ref, far_low_ref, far_high_ref):
    grad = grad_txt_tile(768, low_ref, high_ref, img_ref)
    far_low_ref[0:128, :] = grad[0:128]
    far_high_ref[...] = grad[128:256]
    encode(far_low_ref, 128, scalar_ref[...])


def grad_txt_kernel(low_ref, high_ref, img_ref, *outs):
    step = pl.program_id(0)
    grad = grad_txt_tile(pl.multiple_of(step * 256, 256), low_ref, high_ref, img_ref)
    for k, ref in enumerate(outs):

        @pl.when(step == k)
        def _():
            ref[...] = grad


def finish_kernel(scale_ref, img_ref, txt_ref, img_hat_ref, txt_hat_ref, *refs):
    own_img, ring_img, sib_img, for_sib, own_txt, txt1, txt2, txt3, col_ref, row_ref = refs[:10]
    grad_img_ref, grad_txt_ref, loss_ref, slope_ref = refs[10:]
    scale = scale_ref[0]
    for raw, other, parts, out in (
        (img_ref, txt_hat_ref, (own_img, ring_img, sib_img), grad_img_ref),
        (txt_ref, img_hat_ref, (own_txt, txt1, txt2, txt3), grad_txt_ref),
    ):
        unit, recip = unit_rows(raw)
        total = sum(part[0:64, :].astype(F32) for part in parts)
        grad_hat = scale * (total - other[...].astype(F32))
        inner = jnp.sum(grad_hat * unit, axis=1, keepdims=True)
        out[...] = (recip * (grad_hat - unit * inner)).astype(BF16)
    cols = col_ref[...] + decode(for_sib, 64) + decode(sib_img, 64)
    rows = row_ref[...] + decode(txt1, 64) + decode(txt2, 64) + decode(txt3, 64)
    batch = ROWS * GROUP * GROUP
    diag_sum = scale * rows[0, 2]
    logs = cols[0, 0] + rows[0, 0] + 2.0 * batch * scale_ref[1]
    loss_ref[0] = (logs - 2.0 * diag_sum) / (2 * batch)
    slope_ref[0] = (scale * (cols[0, 1] + rows[0, 1]) - diag_sum) / batch


def places():
    y, z, core = lax.axis_index("y"), lax.axis_index("z"), lax.axis_index("c")
    x = 2 * lax.axis_index("xh") + lax.axis_index("xl")
    near = jnp.array([0, 3, 1, 2], jnp.int32)
    first, second = jnp.tile(near, 4), jnp.repeat(near, 4)
    on_x = jnp.where(core == 0, first, second)
    on_y = jnp.where(core == 0, second, first)
    cols = ((y + on_y) % 4) * 4 + (x + on_x) % 4
    distance = jnp.array([-1, -1, -2, -2, -3, -3, -4, 0, 1, 1, 2, 2, 3, 3, 4, 0], jnp.int32)
    others = jnp.array([1, 0, 1, 0, 1, 0, 1, 1, 0, 1, 0, 1, 0, 1, 0, 0], jnp.int32)
    way = jnp.where(core == 0, -1, 1)
    rows = ((core + others) % 2) * 8 + (z + way * distance) % 8
    return rows.astype(jnp.int32), cols.astype(jnp.int32)


def per_device(image_raw, text_raw, log_scale):
    rows, width = image_raw.shape
    total = rows * GROUP
    img_hat = call(normalize_kernel, shape(rows, width), [VMEM], "normalize_img")(image_raw)
    txt_hat = call(normalize_kernel, shape(rows, width), [VMEM], "normalize_txt")(text_raw)
    diag = call(diagonal_kernel, shape(8, 128, dtype=F32), [VMEM] * 2, "diagonal")(img_hat, txt_hat)

    scale = jnp.exp(log_scale[0])
    shift = jnp.maximum(1.01 * scale - 70.0, 0.0)
    scales = jnp.stack([scale, shift, scale * LOG2_E, shift * LOG2_E])
    row_place, col_place = places()

    sib = to_sibling(img_hat)
    below, above, far = first_axis(txt_hat, 1), first_axis(txt_hat, -1), first_axis(txt_hat, 2)
    ring1 = ring(jnp.concatenate([img_hat, sib], axis=0), 1)
    line = jnp.concatenate([txt_hat, below, above, far], axis=0)
    up, down = second_axis(line, 1), second_axis(line, -1)
    ring1, _ = lax.optimization_barrier((ring1, line))
    ring2 = ring(ring1, 1)
    low_far, high_far = second_axis(up[:128], 1), second_axis(down[128:], -1)
    ring3 = ring(ring2, 1)
    ring3, _, _ = lax.optimization_barrier((ring3, up, down))
    ring4 = ring(ring3, 1)
    img_blocks = [to_sibling(block) for block in (ring1, ring2, ring3)] + [sib, ring1, ring2, ring3, ring4, img_hat]
    img_order = [(0, 0, 128), (1, 0, 128), (2, 0, 128), (7, 64, 64), (3, 0, 64)]
    img_order += [(4, 0, 128), (5, 0, 128), (6, 0, 128), (7, 0, 64), (8, 0, 64)]
    txt_blocks = [line, up, down, low_far, high_far]
    txt_order = [(k, 0, block.shape[0]) for k, block in enumerate(txt_blocks)]

    flops = 2 * total * total * width
    img_all, txt_all, logits, row_part, col_part = call(
        lambda *refs: logits_kernel(img_order, txt_order, *refs),
        (
            shape(total, width),
            shape(total, width),
            shape(total, total, dtype=F32),
            shape(24, 128, dtype=F32),
            shape(16, 128, dtype=F32),
        ),
        [SMEM] * 3 + [VMEM] * (1 + len(img_blocks) + len(txt_blocks)),
        "logits",
        flops,
    )(row_place, col_place, scales, diag, *img_blocks, *txt_blocks)

    row_pair = row_part + to_sibling(row_part)
    col_line = col_part + along(col_part, "x", 1) + along(col_part, "x", 2) + along(col_part, "x", 3)
    lower, upper = along(row_pair, "z", 1), along(row_pair, "z", -1)
    two = row_pair + lower
    three = two + upper
    row_parts = [three, along(three, "z", 3), along(two, "z", -3)]
    col_parts = [col_line] + [along(col_line, "y", k) for k in (1, 2, 3)]

    eight = shape(8, 128, dtype=F32)
    half_grad = (shape(total // 2 + 16, width), shape(total // 2, total))
    send, dlogits_low, row_half, col_half, row_scalars, col_scalars = call(
        grad_img_kernel,
        half_grad + (shape(total, 128, dtype=F32), shape(8, total, dtype=F32), eight, eight),
        [SMEM] * 3 + [VMEM] * 9,
        "grad_img",
        flops // 2,
        scratch_shapes=[pltpu.VMEM((24, 128), F32), pltpu.VMEM((16, 128), F32)],
    )(row_place, col_place, scales, logits, txt_all, *row_parts, *col_parts)
    arrived = to_sibling(send)
    keep, dlogits_high = call(
        grad_img_rest_kernel,
        half_grad,
        [SMEM] + [VMEM] * 5,
        "grad_img_rest",
        flops // 2,
    )(scales, logits, txt_all, row_half, col_half, col_scalars)
    core = jnp.reshape(lax.axis_index("c"), (1,)).astype(jnp.int32)
    far, rest, own_img, col_scalars = call(
        pair_kernel,
        (shape(80, width), shape(384, width), shape(64, width), shape(8, 128, dtype=F32)),
        [SMEM] + [VMEM] * 2,
        "pair",
    )(core, keep, arrived)
    ring1 = ring(far, -1)
    far_low, far_high = call(
        grad_txt_far_kernel,
        (shape(144, width), shape(128, width)),
        [VMEM] * 4,
        "grad_txt_far",
        flops // 4,
    )(dlogits_low, dlogits_high, img_all, row_scalars)
    low, high = second_axis(far_low, -1), second_axis(far_high, 1)
    txt_own, txt_minus, txt_plus = call(
        grad_txt_kernel,
        (shape(256, width),) * 3,
        [VMEM] * 3,
        "grad_txt",
        flops // 4 * 3,
        grid=(3,),
        out_specs=(VMEM,) * 3,
    )(dlogits_low, dlogits_high, img_all)

    def ring_fold(start, arrived):
        return call(
            lambda *refs: ring_fold_kernel(start, *refs), shape(144, width), [VMEM] * 3, "ring_fold"
        )(rest, arrived, col_scalars)

    ring1, _ = lax.optimization_barrier((ring1, txt_own))
    ring2 = ring(ring_fold(256, ring1), -1)
    to_minus, to_plus = call(
        plane_fold_kernel, (shape(272, width),) * 2, [VMEM] * 5, "plane_fold"
    )(txt_minus, txt_plus, low, high, row_scalars)
    down, up = second_axis(to_minus, -1), second_axis(to_plus, 1)
    ring2, _ = lax.optimization_barrier((ring2, to_plus))
    ring3 = ring(ring_fold(128, ring2), -1)
    own_txt, *sends, row_scalars = call(
        line_kernel,
        (shape(64, width),) + (shape(80, width),) * 3 + (shape(8, 128, dtype=F32),),
        [VMEM] * 4,
        "line",
    )(txt_own, down, up, row_scalars)
    to_own, to_sib = call(
        last_fold_kernel, (shape(64, width), shape(80, width)), [VMEM] * 3, "last_fold"
    )(rest, ring3, col_scalars)
    for_sib = ring(to_sib, -1)
    txt_parts = [own_txt] + [first_axis(part, step) for part, step in zip(sends, (-1, 1, 2))]
    img_parts = [own_img, ring(to_own, -1), to_sibling(for_sib), for_sib]

    scalar = shape(1, dtype=F32)
    return call(
        finish_kernel,
        (shape(rows, width), shape(rows, width), scalar, scalar),
        [SMEM] + [VMEM] * 14,
        "finish",
        out_specs=(VMEM, VMEM, SMEM, SMEM),
    )(scales, image_raw, text_raw, img_hat, txt_hat, *img_parts, *txt_parts, col_scalars, row_scalars)


def solution(mesh):
    mesh = Mesh(mesh.devices.reshape(SIZES), AXES)
    spec = P(AXES, None)
    return jax.shard_map(
        per_device, mesh=mesh, in_specs=(spec, spec, P()), out_specs=(spec, spec, P(), P()), check_vma=False
    )
```

```python
import itertools

import jax
import jax.numpy as jnp
from jax import lax
from jax.experimental import pallas as pl
from jax.experimental.pallas import tpu as pltpu
from jax.sharding import Mesh, PartitionSpec as P

NORM_EPS = 1e-06
LOG2_E = 1.4426950408889634
AXES = ("y", "xh", "c", "xl", "z")
SIZES = (4, 2, 2, 2, 8)
GROUP = 16
ROWS = 64
VMEM_LIMIT = 24 * 1024 * 1024
F32 = jnp.float32
BF16 = jnp.bfloat16
VMEM = pl.BlockSpec(memory_space=pltpu.VMEM)
SMEM = pl.BlockSpec(memory_space=pltpu.SMEM)


def call(kernel, out, ins, name, flops=0, **more):
    return pl.pallas_call(
        kernel,
        out_shape=out,
        in_specs=ins,
        compiler_params=pltpu.CompilerParams(vmem_limit_bytes=VMEM_LIMIT),
        cost_estimate=pl.CostEstimate(flops=flops, bytes_accessed=1 << 20, transcendentals=0),
        name=name,
        **more,
    )


def shape(*dims, dtype=BF16):
    return jax.ShapeDtypeStruct(dims, dtype)


def permute(array, move):
    flat = lambda x, y, z, c: (((y * 2 + x // 2) * 2 + c) * 2 + x % 2) * 8 + z
    pairs = []
    for y, xh, c, xl, z in itertools.product(*map(range, SIZES)):
        x2, y2, z2, c2 = move(2 * xh + xl, y, z, c)
        pairs.append((flat(2 * xh + xl, y, z, c), flat(x2 % 4, y2 % 4, z2 % 8, c2 % 2)))
    return lax.ppermute(array, AXES, pairs)


def to_sibling(array):
    return permute(array, lambda x, y, z, c: (x, y, z, 1 - c))


def along(array, axis, step):
    steps = {"x": (step, 0, 0), "y": (0, step, 0), "z": (0, 0, step)}[axis]
    return permute(array, lambda x, y, z, c: (x + steps[0], y + steps[1], z + steps[2], c))


def first_axis(array, step):
    return permute(array, lambda x, y, z, c: (x + step, y, z, c) if c == 0 else (x, y + step, z, c))


def second_axis(array, step):
    return permute(array, lambda x, y, z, c: (x, y + step, z, c) if c == 0 else (x + step, y, z, c))


def ring(array, step):
    return permute(array, lambda x, y, z, c: (x, y, z + (step if c == 0 else -step), c))


def unit_rows(ref):
    values = ref[...].astype(F32)
    recip = 1.0 / jnp.sqrt(jnp.sum(values * values, axis=1, keepdims=True) + NORM_EPS)
    return values * recip, recip


def normalize_kernel(raw_ref, hat_ref):
    hat_ref[...] = unit_rows(raw_ref)[0].astype(BF16)


def diagonal_kernel(img_hat_ref, txt_hat_ref, diag_ref):
    products = img_hat_ref[...].astype(F32) * txt_hat_ref[...].astype(F32)
    diag_ref[...] = jnp.full(diag_ref.shape, jnp.sum(products), F32)


def encode(ref, at, scalars):
    high = scalars.astype(BF16).astype(F32)
    middle = (scalars - high).astype(BF16).astype(F32)
    parts = (high, middle, scalars - high - middle)
    row = lax.broadcasted_iota(jnp.int32, (16, 128), 0)
    block = jnp.zeros((16, 128), F32)
    for k, part in enumerate(parts):
        block = jnp.where(row == k, jnp.concatenate([part, part], axis=0), block)
    ref[at : at + 16, 0:128] = block.astype(BF16)
    ref[at : at + 16, 128:] = jnp.zeros((16, ref.shape[1] - 128), BF16)


def decode(ref, at):
    block = ref[at : at + 16, 0:128].astype(F32)
    return jnp.broadcast_to(jnp.sum(block, axis=0, keepdims=True), (8, 128))


def pair_kernel(core_ref, keep_ref, arrived_ref, far_ref, rest_ref, own_ref, scalar_ref):
    total = keep_ref[0:512, :].astype(F32) + arrived_ref[0:512, :].astype(F32)
    total = total.astype(BF16)
    rest_ref[...] = total[0:384]
    far_ref[0:64, :] = total[384:448]
    own_ref[...] = total[448:512]
    scalars = decode(keep_ref, 512) + decode(arrived_ref, 512)
    scalar_ref[...] = scalars
    encode(far_ref, 64, jnp.where(core_ref[0] == 0, scalars, 0.0))


def ring_fold_kernel(start, base_ref, arrived_ref, scalar_ref, out_ref):
    rows = arrived_ref.shape[0] - 16
    out_ref[0:rows, :] = (
        base_ref[start : start + rows, :].astype(F32) + arrived_ref[0:rows, :].astype(F32)
    ).astype(BF16)
    if rows < 128:
        out_ref[rows:128, :] = base_ref[start + rows : start + 128, :]
    encode(out_ref, 128, scalar_ref[...] + decode(arrived_ref, rows))


def last_fold_kernel(base_ref, arrived_ref, scalar_ref, own_ref, sib_ref):
    for k, out in enumerate((own_ref, sib_ref)):
        cut = slice(k * 64, (k + 1) * 64)
        out[0:64, :] = (base_ref[cut, :].astype(F32) + arrived_ref[cut, :].astype(F32)).astype(BF16)
    encode(sib_ref, 64, scalar_ref[...] + decode(arrived_ref, 128))


def plane_fold_kernel(minus_ref, plus_ref, low_ref, high_ref, scalar_ref, to_minus_ref, to_plus_ref):
    to_minus_ref[0:128, :] = (minus_ref[0:128, :].astype(F32) + low_ref[0:128, :].astype(F32)).astype(BF16)
    to_minus_ref[128:256, :] = minus_ref[128:256, :]
    to_plus_ref[0:128, :] = plus_ref[0:128, :]
    to_plus_ref[128:256, :] = (plus_ref[128:256, :].astype(F32) + high_ref[...].astype(F32)).astype(BF16)
    encode(to_minus_ref, 256, scalar_ref[...] + decode(low_ref, 128))
    encode(to_plus_ref, 256, scalar_ref[...])


def line_kernel(own_ref, down_ref, up_ref, scalar_ref, *outs):
    scalars = scalar_ref[...] + decode(down_ref, 256) + decode(up_ref, 256)
    for k, out in enumerate(outs[:4]):
        cut = slice(k * 64, (k + 1) * 64)
        out[0:64, :] = (
            own_ref[cut, :].astype(F32) + down_ref[cut, :].astype(F32) + up_ref[cut, :].astype(F32)
        ).astype(BF16)
        if k:
            encode(out, 64, scalars)
    outs[4][...] = scalars


def copy_rows(source, first, target, at, rows):
    @pl.loop(0, rows // 32)
    def _(k):
        cut = pl.ds(pl.multiple_of(first + k * 32, 32), 32)
        target[pl.ds(pl.multiple_of(at + k * 32, 32), 32), :] = source[cut, :]


def txt_tile(refs, step):
    if step < 3:
        return refs[step][...]
    return jnp.concatenate([refs[3][...], refs[4][...]], axis=0)


def gather_txt_kernel(*refs):
    at = 0
    for ref in refs[:-1]:
        copy_rows(ref, 0, refs[-1], at, ref.shape[0])
        at += ref.shape[0]


def logits_kernel(img_order, *refs):
    row_place, col_place, scale_ref, diag_ref = refs[:4]
    n_img, n_txt = 9, 5
    img_refs, txt_refs = refs[4 : 4 + n_img], refs[4 + n_img : 4 + n_img + n_txt]
    img_all, logit_ref, row_ref, col_ref = refs[4 + n_img + n_txt :]
    tile = 256
    at = 0
    for k, first, size in img_order:
        copy_rows(img_refs[k], first, img_all, at, size)
        at += size
    row_sums, row_slopes = [], []
    for step in range(4):
        cut = slice(step * tile, (step + 1) * tile)
        logits = lax.dot_general(
            img_all[...], txt_tile(txt_refs, step), (((1,), (1,)), ((), ())), preferred_element_type=F32
        )
        logit_ref[:, cut] = logits
        powers = jnp.exp2(logits * scale_ref[2] - scale_ref[3])
        weighted = powers * logits
        row_sums.append(powers[:, 0:128] + powers[:, 128:256])
        row_slopes.append(weighted[:, 0:128] + weighted[:, 128:256])
        sums = jnp.sum(powers, axis=0, keepdims=True)
        slopes = jnp.sum(weighted, axis=0, keepdims=True)
        for k in range(tile // 64):
            at = col_place[step * (tile // 64) + k]
            part = slice(k * 64, (k + 1) * 64)
            col_ref[pl.ds(at, 1), :] = jnp.concatenate([sums[:, part], slopes[:, part]], axis=1)
    sums = jnp.sum(sum(row_sums).T, axis=0, keepdims=True)
    slopes = jnp.sum(sum(row_slopes).T, axis=0, keepdims=True)
    for k in range(GROUP):
        part = slice(k * 64, (k + 1) * 64)
        row_ref[pl.ds(row_place[k], 1), :] = jnp.concatenate([sums[:, part], slopes[:, part]], axis=1)
    row_ref[16:24, :] = diag_ref[...]


def grad_img_tiles(half, scale_ref, logit_ref, txt_ref, row_half, col_half, grad_ref, dlogit_ref):
    @pl.loop(0, 2)
    def _(step):
        cut = pl.ds(pl.multiple_of(step * 256, 256), 256)
        rows = pl.ds(pl.multiple_of(half * 512 + step * 256, 256), 256)
        powers = jnp.exp2(logit_ref[rows, :] * scale_ref[2] - scale_ref[3])
        by_row = jnp.concatenate([row_half[rows, :]] * 8, axis=1)
        dlogit = (powers * (by_row + col_half[0:1, :])).astype(BF16)
        dlogit_ref[cut, :] = dlogit
        grad_ref[cut, :] = jnp.dot(dlogit, txt_ref[...], preferred_element_type=F32).astype(BF16)


def grad_img_columns(half, scale_ref, logit_ref, txt_ref, row_half, col_half, grad_ref, dlogit_ref):
    rows = slice(half * 512, (half + 1) * 512)
    powers = jnp.exp2(logit_ref[rows, :] * scale_ref[2] - scale_ref[3])
    by_row = jnp.concatenate([row_half[rows, :]] * 8, axis=1)
    dlogit_ref[...] = (powers * (by_row + col_half[0:1, :])).astype(BF16)

    @pl.loop(0, 5)
    def _(step):
        cut = pl.ds(pl.multiple_of(step * 256, 256), 256)
        grad = jnp.dot(dlogit_ref[...], txt_ref[:, cut], preferred_element_type=F32)
        grad_ref[0:512, cut] = grad.astype(BF16)


def grad_img_kernel(*refs):
    row_place, col_place, scale_ref, logit_ref, txt_ref = refs[:5]
    rows_in, cols_in = refs[5:8], refs[8:12]
    grad_ref, dlogit_ref, row_half, col_half, row_scalars, col_scalars = refs[12:-2]
    row_sum, col_sum = refs[-2:]
    row_sum[...] = rows_in[0][...] + rows_in[1][...] + rows_in[2][...]
    col_sum[...] = cols_in[0][...] + cols_in[1][...] + cols_in[2][...] + cols_in[3][...]
    row = jnp.concatenate([row_sum[pl.ds(row_place[k], 1), 0:64] for k in range(16)], axis=1)
    col = jnp.concatenate([col_sum[pl.ds(col_place[k], 1), 0:64] for k in range(16)], axis=1)
    row_half[...] = jnp.broadcast_to(0.5 / row, (128, 1024)).T
    col_half[...] = jnp.broadcast_to(0.5 / col, (8, 1024))
    lane = lax.broadcasted_iota(jnp.int32, (8, 128), 1)

    def scalars(sums, last):
        log_sum = jnp.sum(jnp.log(sums[0:16, 0:64]))
        slope = 0.5 * jnp.sum(sums[0:16, 64:128] / sums[0:16, 0:64])
        return jnp.where(lane == 0, log_sum, jnp.where(lane == 1, slope, last))

    row_scalars[...] = scalars(row_sum, row_sum[16:24, :])
    col_scalars[...] = scalars(col_sum, 0.0)
    encode(grad_ref, 512, col_scalars[...])
    grad_img_tiles(0, scale_ref, logit_ref, txt_ref, row_half, col_half, grad_ref, dlogit_ref)


def grad_img_rest_kernel(scale_ref, logit_ref, txt_ref, row_half, col_half, scalar_ref, grad_ref, dlogit_ref):
    encode(grad_ref, 512, scalar_ref[...])
    grad_img_columns(1, scale_ref, logit_ref, txt_ref, row_half, col_half, grad_ref, dlogit_ref)


def grad_txt_tile(start, low_ref, high_ref, img_ref):
    return sum(
        lax.dot_general(
            part[:, pl.ds(start, 256)],
            img_ref[k * 512 : (k + 1) * 512, :],
            (((0,), (0,)), ((), ())),
            preferred_element_type=F32,
        )
        for k, part in enumerate((low_ref, high_ref))
    ).astype(BF16)


def grad_txt_far_kernel(low_ref, high_ref, img_ref, scalar_ref, far_low_ref, far_high_ref):
    grad = grad_txt_tile(768, low_ref, high_ref, img_ref)
    far_low_ref[0:128, :] = grad[0:128]
    far_high_ref[...] = grad[128:256]
    encode(far_low_ref, 128, scalar_ref[...])


def grad_txt_kernel(low_ref, high_ref, img_ref, *outs):
    step = pl.program_id(0)
    grad = grad_txt_tile(pl.multiple_of(step * 256, 256), low_ref, high_ref, img_ref)
    for k, ref in enumerate(outs):

        @pl.when(step == k)
        def _():
            ref[...] = grad


def finish_kernel(scale_ref, img_ref, txt_ref, img_hat_ref, txt_hat_ref, *refs):
    own_img, ring_img, sib_img, for_sib, own_txt, txt1, txt2, txt3, col_ref, row_ref = refs[:10]
    grad_img_ref, grad_txt_ref, loss_ref, slope_ref = refs[10:]
    scale = scale_ref[0]
    for raw, other, parts, out in (
        (img_ref, txt_hat_ref, (own_img, ring_img, sib_img), grad_img_ref),
        (txt_ref, img_hat_ref, (own_txt, txt1, txt2, txt3), grad_txt_ref),
    ):
        unit, recip = unit_rows(raw)
        total = sum(part[0:64, :].astype(F32) for part in parts)
        grad_hat = scale * (total - other[...].astype(F32))
        inner = jnp.sum(grad_hat * unit, axis=1, keepdims=True)
        out[...] = (recip * (grad_hat - unit * inner)).astype(BF16)
    cols = col_ref[...] + decode(for_sib, 64) + decode(sib_img, 64)
    rows = row_ref[...] + decode(txt1, 64) + decode(txt2, 64) + decode(txt3, 64)
    batch = ROWS * GROUP * GROUP
    diag_sum = scale * rows[0, 2]
    logs = cols[0, 0] + rows[0, 0] + 2.0 * batch * scale_ref[1]
    loss_ref[0] = (logs - 2.0 * diag_sum) / (2 * batch)
    slope_ref[0] = (scale * (cols[0, 1] + rows[0, 1]) - diag_sum) / batch


def places():
    y, z, core = lax.axis_index("y"), lax.axis_index("z"), lax.axis_index("c")
    x = 2 * lax.axis_index("xh") + lax.axis_index("xl")
    near = jnp.array([0, 3, 1, 2], jnp.int32)
    first, second = jnp.tile(near, 4), jnp.repeat(near, 4)
    on_x = jnp.where(core == 0, first, second)
    on_y = jnp.where(core == 0, second, first)
    cols = ((y + on_y) % 4) * 4 + (x + on_x) % 4
    distance = jnp.array([-1, -1, -2, -2, -3, -3, -4, 0, 1, 1, 2, 2, 3, 3, 4, 0], jnp.int32)
    others = jnp.array([1, 0, 1, 0, 1, 0, 1, 1, 0, 1, 0, 1, 0, 1, 0, 0], jnp.int32)
    way = jnp.where(core == 0, -1, 1)
    rows = ((core + others) % 2) * 8 + (z + way * distance) % 8
    return rows.astype(jnp.int32), cols.astype(jnp.int32)


def per_device(image_raw, text_raw, log_scale):
    rows, width = image_raw.shape
    total = rows * GROUP
    img_hat = call(normalize_kernel, shape(rows, width), [VMEM], "normalize_img")(image_raw)
    txt_hat = call(normalize_kernel, shape(rows, width), [VMEM], "normalize_txt")(text_raw)
    diag = call(diagonal_kernel, shape(8, 128, dtype=F32), [VMEM] * 2, "diagonal")(img_hat, txt_hat)

    scale = jnp.exp(log_scale[0])
    shift = jnp.maximum(1.01 * scale - 70.0, 0.0)
    scales = jnp.stack([scale, shift, scale * LOG2_E, shift * LOG2_E])
    row_place, col_place = places()

    sib = to_sibling(img_hat)
    below, above, far = first_axis(txt_hat, 1), first_axis(txt_hat, -1), first_axis(txt_hat, 2)
    ring1 = ring(jnp.concatenate([img_hat, sib], axis=0), 1)
    line = jnp.concatenate([txt_hat, below, above, far], axis=0)
    up, down = second_axis(line, 1), second_axis(line, -1)
    ring1, _ = lax.optimization_barrier((ring1, line))
    ring2 = ring(ring1, 1)
    low_far, high_far = second_axis(up[:128], 1), second_axis(down[128:], -1)
    ring3 = ring(ring2, 1)
    ring3, _, _ = lax.optimization_barrier((ring3, up, down))
    ring4 = ring(ring3, 1)
    img_blocks = [to_sibling(block) for block in (ring1, ring2, ring3)] + [sib, ring1, ring2, ring3, ring4, img_hat]
    img_order = [(0, 0, 128), (1, 0, 128), (2, 0, 128), (7, 64, 64), (3, 0, 64)]
    img_order += [(4, 0, 128), (5, 0, 128), (6, 0, 128), (7, 0, 64), (8, 0, 64)]
    txt_blocks = [line, up, down, low_far, high_far]

    flops = 2 * total * total * width
    img_all, logits, row_part, col_part = call(
        lambda *refs: logits_kernel(img_order, *refs),
        (
            shape(total, width),
            shape(total, total, dtype=F32),
            shape(24, 128, dtype=F32),
            shape(16, 128, dtype=F32),
        ),
        [SMEM] * 3 + [VMEM] * (1 + len(img_blocks) + len(txt_blocks)),
        "logits",
        flops,
    )(row_place, col_place, scales, diag, *img_blocks, *txt_blocks)
    txt_all = call(gather_txt_kernel, shape(total, width), [VMEM] * len(txt_blocks), "gather_txt")(*txt_blocks)

    row_pair = row_part + to_sibling(row_part)
    col_line = col_part + along(col_part, "x", 1) + along(col_part, "x", 2) + along(col_part, "x", 3)
    lower, upper = along(row_pair, "z", 1), along(row_pair, "z", -1)
    two = row_pair + lower
    three = two + upper
    row_parts = [three, along(three, "z", 3), along(two, "z", -3)]
    col_parts = [col_line] + [along(col_line, "y", k) for k in (1, 2, 3)]

    eight = shape(8, 128, dtype=F32)
    half_grad = (shape(total // 2 + 16, width), shape(total // 2, total))
    send, dlogits_low, row_half, col_half, row_scalars, col_scalars = call(
        grad_img_kernel,
        half_grad + (shape(total, 128, dtype=F32), shape(8, total, dtype=F32), eight, eight),
        [SMEM] * 3 + [VMEM] * 9,
        "grad_img",
        flops // 2,
        scratch_shapes=[pltpu.VMEM((24, 128), F32), pltpu.VMEM((16, 128), F32)],
    )(row_place, col_place, scales, logits, txt_all, *row_parts, *col_parts)
    arrived = to_sibling(send)
    keep, dlogits_high = call(
        grad_img_rest_kernel,
        half_grad,
        [SMEM] + [VMEM] * 5,
        "grad_img_rest",
        flops // 2,
    )(scales, logits, txt_all, row_half, col_half, col_scalars)
    core = jnp.reshape(lax.axis_index("c"), (1,)).astype(jnp.int32)
    far, rest, own_img, col_scalars = call(
        pair_kernel,
        (shape(80, width), shape(384, width), shape(64, width), shape(8, 128, dtype=F32)),
        [SMEM] + [VMEM] * 2,
        "pair",
    )(core, keep, arrived)
    ring1 = ring(far, -1)
    far_low, far_high = call(
        grad_txt_far_kernel,
        (shape(144, width), shape(128, width)),
        [VMEM] * 4,
        "grad_txt_far",
        flops // 4,
    )(dlogits_low, dlogits_high, img_all, row_scalars)
    low, high = second_axis(far_low, -1), second_axis(far_high, 1)
    txt_own, txt_minus, txt_plus = call(
        grad_txt_kernel,
        (shape(256, width),) * 3,
        [VMEM] * 3,
        "grad_txt",
        flops // 4 * 3,
        grid=(3,),
        out_specs=(VMEM,) * 3,
    )(dlogits_low, dlogits_high, img_all)

    def ring_fold(start, arrived):
        return call(
            lambda *refs: ring_fold_kernel(start, *refs), shape(144, width), [VMEM] * 3, "ring_fold"
        )(rest, arrived, col_scalars)

    ring1, _ = lax.optimization_barrier((ring1, txt_own))
    ring2 = ring(ring_fold(256, ring1), -1)
    to_minus, to_plus = call(
        plane_fold_kernel, (shape(272, width),) * 2, [VMEM] * 5, "plane_fold"
    )(txt_minus, txt_plus, low, high, row_scalars)
    down, up = second_axis(to_minus, -1), second_axis(to_plus, 1)
    ring2, _ = lax.optimization_barrier((ring2, to_plus))
    ring3 = ring(ring_fold(128, ring2), -1)
    own_txt, *sends, row_scalars = call(
        line_kernel,
        (shape(64, width),) + (shape(80, width),) * 3 + (shape(8, 128, dtype=F32),),
        [VMEM] * 4,
        "line",
    )(txt_own, down, up, row_scalars)
    to_own, to_sib = call(
        last_fold_kernel, (shape(64, width), shape(80, width)), [VMEM] * 3, "last_fold"
    )(rest, ring3, col_scalars)
    for_sib = ring(to_sib, -1)
    txt_parts = [own_txt] + [first_axis(part, step) for part, step in zip(sends, (-1, 1, 2))]
    img_parts = [own_img, ring(to_own, -1), to_sibling(for_sib), for_sib]

    scalar = shape(1, dtype=F32)
    return call(
        finish_kernel,
        (shape(rows, width), shape(rows, width), scalar, scalar),
        [SMEM] + [VMEM] * 14,
        "finish",
        out_specs=(VMEM, VMEM, SMEM, SMEM),
    )(scales, image_raw, text_raw, img_hat, txt_hat, *img_parts, *txt_parts, col_scalars, row_scalars)


def solution(mesh):
    mesh = Mesh(mesh.devices.reshape(SIZES), AXES)
    spec = P(AXES, None)
    return jax.shard_map(
        per_device, mesh=mesh, in_specs=(spec, spec, P()), out_specs=(spec, spec, P(), P()), check_vma=False
    )
```

```python
import itertools

import jax
import jax.numpy as jnp
from jax import lax
from jax.experimental import pallas as pl
from jax.experimental.pallas import tpu as pltpu
from jax.sharding import Mesh, PartitionSpec as P

NORM_EPS = 1e-06
LOG2_E = 1.4426950408889634
AXES = ("y", "xh", "c", "xl", "z")
SIZES = (4, 2, 2, 2, 8)
GROUP = 16
ROWS = 64
VMEM_LIMIT = 24 * 1024 * 1024
F32 = jnp.float32
BF16 = jnp.bfloat16
VMEM = pl.BlockSpec(memory_space=pltpu.VMEM)
SMEM = pl.BlockSpec(memory_space=pltpu.SMEM)


def call(kernel, out, ins, name, flops=0, **more):
    return pl.pallas_call(
        kernel,
        out_shape=out,
        in_specs=ins,
        compiler_params=pltpu.CompilerParams(vmem_limit_bytes=VMEM_LIMIT),
        cost_estimate=pl.CostEstimate(flops=flops, bytes_accessed=1 << 20, transcendentals=0),
        name=name,
        **more,
    )


def shape(*dims, dtype=BF16):
    return jax.ShapeDtypeStruct(dims, dtype)


def permute(array, move):
    flat = lambda x, y, z, c: (((y * 2 + x // 2) * 2 + c) * 2 + x % 2) * 8 + z
    pairs = []
    for y, xh, c, xl, z in itertools.product(*map(range, SIZES)):
        x2, y2, z2, c2 = move(2 * xh + xl, y, z, c)
        pairs.append((flat(2 * xh + xl, y, z, c), flat(x2 % 4, y2 % 4, z2 % 8, c2 % 2)))
    return lax.ppermute(array, AXES, pairs)


def to_sibling(array):
    return permute(array, lambda x, y, z, c: (x, y, z, 1 - c))


def along(array, axis, step):
    steps = {"x": (step, 0, 0), "y": (0, step, 0), "z": (0, 0, step)}[axis]
    return permute(array, lambda x, y, z, c: (x + steps[0], y + steps[1], z + steps[2], c))


def first_axis(array, step):
    return permute(array, lambda x, y, z, c: (x + step, y, z, c) if c == 0 else (x, y + step, z, c))


def second_axis(array, step):
    return permute(array, lambda x, y, z, c: (x, y + step, z, c) if c == 0 else (x + step, y, z, c))


def ring(array, step):
    return permute(array, lambda x, y, z, c: (x, y, z + (step if c == 0 else -step), c))


def unit_rows(ref):
    values = ref[...].astype(F32)
    recip = 1.0 / jnp.sqrt(jnp.sum(values * values, axis=1, keepdims=True) + NORM_EPS)
    return values * recip, recip


def normalize_kernel(raw_ref, hat_ref):
    hat_ref[...] = unit_rows(raw_ref)[0].astype(BF16)


def units_kernel(img_raw_ref, txt_raw_ref, img_hat_ref, txt_hat_ref, diag_ref, *outs):
    for raw_ref, unit_ref, recip_ref in ((img_raw_ref, *outs[:2]), (txt_raw_ref, *outs[2:])):
        unit, recip = unit_rows(raw_ref)
        unit_ref[...] = unit
        recip_ref[...] = jnp.broadcast_to(recip, recip_ref.shape)
    products = img_hat_ref[...].astype(F32) * txt_hat_ref[...].astype(F32)
    diag_ref[...] = jnp.full(diag_ref.shape, jnp.sum(products), F32)


def encode(ref, at, scalars):
    high = scalars.astype(BF16).astype(F32)
    middle = (scalars - high).astype(BF16).astype(F32)
    parts = (high, middle, scalars - high - middle)
    row = lax.broadcasted_iota(jnp.int32, (16, 128), 0)
    block = jnp.zeros((16, 128), F32)
    for k, part in enumerate(parts):
        block = jnp.where(row == k, jnp.concatenate([part, part], axis=0), block)
    ref[at : at + 16, 0:128] = block.astype(BF16)
    ref[at : at + 16, 128:] = jnp.zeros((16, ref.shape[1] - 128), BF16)


def decode(ref, at):
    block = ref[at : at + 16, 0:128].astype(F32)
    return jnp.broadcast_to(jnp.sum(block, axis=0, keepdims=True), (8, 128))


def pair_kernel(core_ref, keep_ref, arrived_ref, far_ref, rest_ref, own_ref, scalar_ref):
    total = keep_ref[0:512, :].astype(F32) + arrived_ref[0:512, :].astype(F32)
    total = total.astype(BF16)
    rest_ref[...] = total[0:384]
    far_ref[0:64, :] = total[384:448]
    own_ref[...] = total[448:512]
    scalars = decode(keep_ref, 512) + decode(arrived_ref, 512)
    scalar_ref[...] = scalars
    encode(far_ref, 64, jnp.where(core_ref[0] == 0, scalars, 0.0))


def ring_fold_kernel(start, base_ref, arrived_ref, scalar_ref, out_ref):
    rows = arrived_ref.shape[0] - 16
    out_ref[0:rows, :] = (
        base_ref[start : start + rows, :].astype(F32) + arrived_ref[0:rows, :].astype(F32)
    ).astype(BF16)
    if rows < 128:
        out_ref[rows:128, :] = base_ref[start + rows : start + 128, :]
    encode(out_ref, 128, scalar_ref[...] + decode(arrived_ref, rows))


def last_fold_kernel(base_ref, arrived_ref, scalar_ref, own_ref, sib_ref):
    for k, out in enumerate((own_ref, sib_ref)):
        cut = slice(k * 64, (k + 1) * 64)
        out[0:64, :] = (base_ref[cut, :].astype(F32) + arrived_ref[cut, :].astype(F32)).astype(BF16)
    encode(sib_ref, 64, scalar_ref[...] + decode(arrived_ref, 128))


def plane_fold_kernel(minus_ref, plus_ref, low_ref, high_ref, scalar_ref, to_minus_ref, to_plus_ref):
    to_minus_ref[0:128, :] = (minus_ref[0:128, :].astype(F32) + low_ref[0:128, :].astype(F32)).astype(BF16)
    to_minus_ref[128:256, :] = minus_ref[128:256, :]
    to_plus_ref[0:128, :] = plus_ref[0:128, :]
    to_plus_ref[128:256, :] = (plus_ref[128:256, :].astype(F32) + high_ref[...].astype(F32)).astype(BF16)
    encode(to_minus_ref, 256, scalar_ref[...] + decode(low_ref, 128))
    encode(to_plus_ref, 256, scalar_ref[...])


def line_kernel(own_ref, down_ref, up_ref, scalar_ref, *outs):
    scalars = scalar_ref[...] + decode(down_ref, 256) + decode(up_ref, 256)
    for k, out in enumerate(outs[:4]):
        cut = slice(k * 64, (k + 1) * 64)
        out[0:64, :] = (
            own_ref[cut, :].astype(F32) + down_ref[cut, :].astype(F32) + up_ref[cut, :].astype(F32)
        ).astype(BF16)
        if k:
            encode(out, 64, scalars)
    outs[4][...] = scalars


def copy_rows(source, first, target, at, rows):
    @pl.loop(0, rows // 32)
    def _(k):
        cut = pl.ds(pl.multiple_of(first + k * 32, 32), 32)
        target[pl.ds(pl.multiple_of(at + k * 32, 32), 32), :] = source[cut, :]


def txt_tile(refs, step):
    if step < 3:
        return refs[step][...]
    return jnp.concatenate([refs[3][...], refs[4][...]], axis=0)


def gather_txt_kernel(*refs):
    at = 0
    for ref in refs[:-1]:
        copy_rows(ref, 0, refs[-1], at, ref.shape[0])
        at += ref.shape[0]


def logits_kernel(img_order, *refs):
    row_place, col_place, scale_ref, diag_ref = refs[:4]
    n_img, n_txt = 9, 5
    img_refs, txt_refs = refs[4 : 4 + n_img], refs[4 + n_img : 4 + n_img + n_txt]
    img_all, logit_ref, row_ref, col_ref = refs[4 + n_img + n_txt :]
    tile = 256
    at = 0
    for k, first, size in img_order:
        copy_rows(img_refs[k], first, img_all, at, size)
        at += size
    row_sums, row_slopes = [], []
    for step in range(4):
        cut = slice(step * tile, (step + 1) * tile)
        logits = lax.dot_general(
            img_all[...], txt_tile(txt_refs, step), (((1,), (1,)), ((), ())), preferred_element_type=F32
        )
        logit_ref[:, cut] = logits
        powers = jnp.exp2(logits * scale_ref[2] - scale_ref[3])
        weighted = powers * logits
        row_sums.append(powers[:, 0:128] + powers[:, 128:256])
        row_slopes.append(weighted[:, 0:128] + weighted[:, 128:256])
        sums = jnp.sum(powers, axis=0, keepdims=True)
        slopes = jnp.sum(weighted, axis=0, keepdims=True)
        for k in range(tile // 64):
            at = col_place[step * (tile // 64) + k]
            part = slice(k * 64, (k + 1) * 64)
            col_ref[pl.ds(at, 1), :] = jnp.concatenate([sums[:, part], slopes[:, part]], axis=1)
    sums = jnp.sum(sum(row_sums).T, axis=0, keepdims=True)
    slopes = jnp.sum(sum(row_slopes).T, axis=0, keepdims=True)
    for k in range(GROUP):
        part = slice(k * 64, (k + 1) * 64)
        row_ref[pl.ds(row_place[k], 1), :] = jnp.concatenate([sums[:, part], slopes[:, part]], axis=1)
    row_ref[16:24, :] = diag_ref[...]


def grad_img_tiles(half, scale_ref, logit_ref, txt_ref, row_half, col_half, grad_ref, dlogit_ref):
    @pl.loop(0, 2)
    def _(step):
        cut = pl.ds(pl.multiple_of(step * 256, 256), 256)
        rows = pl.ds(pl.multiple_of(half * 512 + step * 256, 256), 256)
        powers = jnp.exp2(logit_ref[rows, :] * scale_ref[2] - scale_ref[3])
        by_row = jnp.concatenate([row_half[rows, :]] * 8, axis=1)
        dlogit = (powers * (by_row + col_half[0:1, :])).astype(BF16)
        dlogit_ref[cut, :] = dlogit
        grad_ref[cut, :] = jnp.dot(dlogit, txt_ref[...], preferred_element_type=F32).astype(BF16)


def grad_img_columns(half, scale_ref, logit_ref, txt_ref, row_half, col_half, grad_ref, dlogit_ref):
    rows = slice(half * 512, (half + 1) * 512)
    powers = jnp.exp2(logit_ref[rows, :] * scale_ref[2] - scale_ref[3])
    by_row = jnp.concatenate([row_half[rows, :]] * 8, axis=1)
    dlogit_ref[...] = (powers * (by_row + col_half[0:1, :])).astype(BF16)

    @pl.loop(0, 5)
    def _(step):
        cut = pl.ds(pl.multiple_of(step * 256, 256), 256)
        grad = jnp.dot(dlogit_ref[...], txt_ref[:, cut], preferred_element_type=F32)
        grad_ref[0:512, cut] = grad.astype(BF16)


def grad_img_kernel(*refs):
    row_place, col_place, scale_ref, logit_ref, txt_ref = refs[:5]
    rows_in, cols_in = refs[5:8], refs[8:12]
    grad_ref, dlogit_ref, row_half, col_half, row_scalars, col_scalars = refs[12:-2]
    row_sum, col_sum = refs[-2:]
    row_sum[...] = rows_in[0][...] + rows_in[1][...] + rows_in[2][...]
    col_sum[...] = cols_in[0][...] + cols_in[1][...] + cols_in[2][...] + cols_in[3][...]
    row = jnp.concatenate([row_sum[pl.ds(row_place[k], 1), 0:64] for k in range(16)], axis=1)
    col = jnp.concatenate([col_sum[pl.ds(col_place[k], 1), 0:64] for k in range(16)], axis=1)
    row_half[...] = jnp.broadcast_to(0.5 / row, (128, 1024)).T
    col_half[...] = jnp.broadcast_to(0.5 / col, (8, 1024))
    lane = lax.broadcasted_iota(jnp.int32, (8, 128), 1)

    def scalars(sums, last):
        log_sum = jnp.sum(jnp.log(sums[0:16, 0:64]))
        slope = 0.5 * jnp.sum(sums[0:16, 64:128] / sums[0:16, 0:64])
        return jnp.where(lane == 0, log_sum, jnp.where(lane == 1, slope, last))

    row_scalars[...] = scalars(row_sum, row_sum[16:24, :])
    col_scalars[...] = scalars(col_sum, 0.0)
    encode(grad_ref, 512, col_scalars[...])
    grad_img_tiles(0, scale_ref, logit_ref, txt_ref, row_half, col_half, grad_ref, dlogit_ref)


def grad_img_rest_kernel(scale_ref, logit_ref, txt_ref, row_half, col_half, scalar_ref, grad_ref, dlogit_ref):
    encode(grad_ref, 512, scalar_ref[...])
    grad_img_columns(1, scale_ref, logit_ref, txt_ref, row_half, col_half, grad_ref, dlogit_ref)


def grad_txt_tile(start, low_ref, high_ref, img_ref):
    return sum(
        lax.dot_general(
            part[:, pl.ds(start, 256)],
            img_ref[k * 512 : (k + 1) * 512, :],
            (((0,), (0,)), ((), ())),
            preferred_element_type=F32,
        )
        for k, part in enumerate((low_ref, high_ref))
    ).astype(BF16)


def grad_txt_far_kernel(low_ref, high_ref, img_ref, scalar_ref, far_low_ref, far_high_ref):
    grad = grad_txt_tile(768, low_ref, high_ref, img_ref)
    far_low_ref[0:128, :] = grad[0:128]
    far_high_ref[...] = grad[128:256]
    encode(far_low_ref, 128, scalar_ref[...])


def grad_txt_kernel(low_ref, high_ref, img_ref, *outs):
    step = pl.program_id(0)
    grad = grad_txt_tile(pl.multiple_of(step * 256, 256), low_ref, high_ref, img_ref)
    for k, ref in enumerate(outs):

        @pl.when(step == k)
        def _():
            ref[...] = grad


def finish_kernel(scale_ref, img_ref, img_recip, txt_ref, txt_recip, img_hat_ref, txt_hat_ref, *refs):
    own_img, ring_img, sib_img, for_sib, own_txt, txt1, txt2, txt3, col_ref, row_ref = refs[:10]
    grad_img_ref, grad_txt_ref, loss_ref, slope_ref = refs[10:]
    scale = scale_ref[0]
    for unit_ref, recip_ref, other, parts, out in (
        (img_ref, img_recip, txt_hat_ref, (own_img, ring_img, sib_img), grad_img_ref),
        (txt_ref, txt_recip, img_hat_ref, (own_txt, txt1, txt2, txt3), grad_txt_ref),
    ):
        unit = unit_ref[...]
        total = sum(part[0:64, :].astype(F32) for part in parts)
        grad_hat = scale * (total - other[...].astype(F32))
        inner = jnp.sum(grad_hat * unit, axis=1, keepdims=True)
        recip = jnp.concatenate([recip_ref[...]] * (unit.shape[1] // 128), axis=1)
        out[...] = (recip * (grad_hat - unit * inner)).astype(BF16)
    cols = col_ref[...] + decode(for_sib, 64) + decode(sib_img, 64)
    rows = row_ref[...] + decode(txt1, 64) + decode(txt2, 64) + decode(txt3, 64)
    batch = ROWS * GROUP * GROUP
    diag_sum = scale * rows[0, 2]
    logs = cols[0, 0] + rows[0, 0] + 2.0 * batch * scale_ref[1]
    loss_ref[0] = (logs - 2.0 * diag_sum) / (2 * batch)
    slope_ref[0] = (scale * (cols[0, 1] + rows[0, 1]) - diag_sum) / batch


def places():
    y, z, core = lax.axis_index("y"), lax.axis_index("z"), lax.axis_index("c")
    x = 2 * lax.axis_index("xh") + lax.axis_index("xl")
    near = jnp.array([0, 3, 1, 2], jnp.int32)
    first, second = jnp.tile(near, 4), jnp.repeat(near, 4)
    on_x = jnp.where(core == 0, first, second)
    on_y = jnp.where(core == 0, second, first)
    cols = ((y + on_y) % 4) * 4 + (x + on_x) % 4
    distance = jnp.array([-1, -1, -2, -2, -3, -3, -4, 0, 1, 1, 2, 2, 3, 3, 4, 0], jnp.int32)
    others = jnp.array([1, 0, 1, 0, 1, 0, 1, 1, 0, 1, 0, 1, 0, 1, 0, 0], jnp.int32)
    way = jnp.where(core == 0, -1, 1)
    rows = ((core + others) % 2) * 8 + (z + way * distance) % 8
    return rows.astype(jnp.int32), cols.astype(jnp.int32)


def per_device(image_raw, text_raw, log_scale):
    rows, width = image_raw.shape
    total = rows * GROUP
    img_hat = call(normalize_kernel, shape(rows, width), [VMEM], "normalize_img")(image_raw)
    txt_hat = call(normalize_kernel, shape(rows, width), [VMEM], "normalize_txt")(text_raw)
    unit = (shape(rows, width, dtype=F32), shape(rows, 128, dtype=F32))
    diag, *units = call(units_kernel, (shape(8, 128, dtype=F32), *unit, *unit), [VMEM] * 4, "units")(
        image_raw, text_raw, img_hat, txt_hat
    )

    scale = jnp.exp(log_scale[0])
    shift = jnp.maximum(1.01 * scale - 70.0, 0.0)
    scales = jnp.stack([scale, shift, scale * LOG2_E, shift * LOG2_E])
    row_place, col_place = places()

    sib = to_sibling(img_hat)
    below, above, far = first_axis(txt_hat, 1), first_axis(txt_hat, -1), first_axis(txt_hat, 2)
    ring1 = ring(jnp.concatenate([img_hat, sib], axis=0), 1)
    line = jnp.concatenate([txt_hat, below, above, far], axis=0)
    up, down = second_axis(line, 1), second_axis(line, -1)
    ring1, _ = lax.optimization_barrier((ring1, line))
    ring2 = ring(ring1, 1)
    low_far, high_far = second_axis(up[:128], 1), second_axis(down[128:], -1)
    ring3 = ring(ring2, 1)
    ring3, _, _ = lax.optimization_barrier((ring3, up, down))
    ring4 = ring(ring3, 1)
    img_blocks = [to_sibling(block) for block in (ring1, ring2, ring3)] + [sib, ring1, ring2, ring3, ring4, img_hat]
    img_order = [(0, 0, 128), (1, 0, 128), (2, 0, 128), (7, 64, 64), (3, 0, 64)]
    img_order += [(4, 0, 128), (5, 0, 128), (6, 0, 128), (7, 0, 64), (8, 0, 64)]
    txt_blocks = [line, up, down, low_far, high_far]

    flops = 2 * total * total * width
    img_all, logits, row_part, col_part = call(
        lambda *refs: logits_kernel(img_order, *refs),
        (
            shape(total, width),
            shape(total, total, dtype=F32),
            shape(24, 128, dtype=F32),
            shape(16, 128, dtype=F32),
        ),
        [SMEM] * 3 + [VMEM] * (1 + len(img_blocks) + len(txt_blocks)),
        "logits",
        flops,
    )(row_place, col_place, scales, diag, *img_blocks, *txt_blocks)
    txt_all = call(gather_txt_kernel, shape(total, width), [VMEM] * len(txt_blocks), "gather_txt")(*txt_blocks)

    row_pair = row_part + to_sibling(row_part)
    col_line = col_part + along(col_part, "x", 1) + along(col_part, "x", 2) + along(col_part, "x", 3)
    lower, upper = along(row_pair, "z", 1), along(row_pair, "z", -1)
    two = row_pair + lower
    three = two + upper
    row_parts = [three, along(three, "z", 3), along(two, "z", -3)]
    col_parts = [col_line] + [along(col_line, "y", k) for k in (1, 2, 3)]

    eight = shape(8, 128, dtype=F32)
    half_grad = (shape(total // 2 + 16, width), shape(total // 2, total))
    send, dlogits_low, row_half, col_half, row_scalars, col_scalars = call(
        grad_img_kernel,
        half_grad + (shape(total, 128, dtype=F32), shape(8, total, dtype=F32), eight, eight),
        [SMEM] * 3 + [VMEM] * 9,
        "grad_img",
        flops // 2,
        scratch_shapes=[pltpu.VMEM((24, 128), F32), pltpu.VMEM((16, 128), F32)],
    )(row_place, col_place, scales, logits, txt_all, *row_parts, *col_parts)
    arrived = to_sibling(send)
    keep, dlogits_high = call(
        grad_img_rest_kernel,
        half_grad,
        [SMEM] + [VMEM] * 5,
        "grad_img_rest",
        flops // 2,
    )(scales, logits, txt_all, row_half, col_half, col_scalars)
    core = jnp.reshape(lax.axis_index("c"), (1,)).astype(jnp.int32)
    far, rest, own_img, col_scalars = call(
        pair_kernel,
        (shape(80, width), shape(384, width), shape(64, width), shape(8, 128, dtype=F32)),
        [SMEM] + [VMEM] * 2,
        "pair",
    )(core, keep, arrived)
    ring1 = ring(far, -1)
    far_low, far_high = call(
        grad_txt_far_kernel,
        (shape(144, width), shape(128, width)),
        [VMEM] * 4,
        "grad_txt_far",
        flops // 4,
    )(dlogits_low, dlogits_high, img_all, row_scalars)
    low, high = second_axis(far_low, -1), second_axis(far_high, 1)
    txt_own, txt_minus, txt_plus = call(
        grad_txt_kernel,
        (shape(256, width),) * 3,
        [VMEM] * 3,
        "grad_txt",
        flops // 4 * 3,
        grid=(3,),
        out_specs=(VMEM,) * 3,
    )(dlogits_low, dlogits_high, img_all)

    def ring_fold(start, arrived):
        return call(
            lambda *refs: ring_fold_kernel(start, *refs), shape(144, width), [VMEM] * 3, "ring_fold"
        )(rest, arrived, col_scalars)

    ring1, _ = lax.optimization_barrier((ring1, txt_own))
    ring2 = ring(ring_fold(256, ring1), -1)
    to_minus, to_plus = call(
        plane_fold_kernel, (shape(272, width),) * 2, [VMEM] * 5, "plane_fold"
    )(txt_minus, txt_plus, low, high, row_scalars)
    down, up = second_axis(to_minus, -1), second_axis(to_plus, 1)
    ring2, _ = lax.optimization_barrier((ring2, to_plus))
    ring3 = ring(ring_fold(128, ring2), -1)
    own_txt, *sends, row_scalars = call(
        line_kernel,
        (shape(64, width),) + (shape(80, width),) * 3 + (shape(8, 128, dtype=F32),),
        [VMEM] * 4,
        "line",
    )(txt_own, down, up, row_scalars)
    to_own, to_sib = call(
        last_fold_kernel, (shape(64, width), shape(80, width)), [VMEM] * 3, "last_fold"
    )(rest, ring3, col_scalars)
    for_sib = ring(to_sib, -1)
    txt_parts = [own_txt] + [first_axis(part, step) for part, step in zip(sends, (-1, 1, 2))]
    img_parts = [own_img, ring(to_own, -1), to_sibling(for_sib), for_sib]

    scalar = shape(1, dtype=F32)
    return call(
        finish_kernel,
        (shape(rows, width), shape(rows, width), scalar, scalar),
        [SMEM] + [VMEM] * 16,
        "finish",
        out_specs=(VMEM, VMEM, SMEM, SMEM),
    )(scales, *units, img_hat, txt_hat, *img_parts, *txt_parts, col_scalars, row_scalars)


def solution(mesh):
    mesh = Mesh(mesh.devices.reshape(SIZES), AXES)
    spec = P(AXES, None)
    return jax.shard_map(
        per_device, mesh=mesh, in_specs=(spec, spec, P()), out_specs=(spec, spec, P(), P()), check_vma=False
    )
```
